32 devices in a mesh: section: 2 (over x), dp: 16 (over z, y, core).
Axes of the slice: x: 2, y: 2, z: 4, core: 2. Of those that a mesh axis runs over, the one named last changes fastest.
Arguments:
- tokens: bfloat16 [32768, 768], P('dp'), may hold values from -6 to 6
- cotangent: bfloat16 [32768, 768], P('dp'), may hold values from -6 to 6
- segment_ids: int32 [64, 512], P('dp'), may hold values from 0 to 7, never falling along the last dimension, each value on 1 to 128 neighbouring positions
- feature_ids: int32 [64, 512], P('dp'), may hold values from 0 to 127, never falling along the last dimension, each value on 1 to 8 neighbouring positions
- w_qkv: bfloat16 [2, 768, 2304], P('section'), may hold values from -0.21875 to 0.21875
- w_out: bfloat16 [2, 768, 768], P('section'), may hold values from -0.875 to 0.875
- gain_attn: float32 [2, 768], P('section'), may hold values from 0.5 to 1.5
- shift_attn: float32 [2, 768], P('section'), may hold values from -3 to 3
- w_up: bfloat16 [2, 768, 3072], P('section'), may hold values from -0.21875 to 0.21875
- bias_up: float32 [2, 3072], P('section'), may hold values from -3 to 3
- w_down: bfloat16 [2, 3072, 768], P('section'), may hold values from -0.109375 to 0.109375
- bias_down: float32 [2, 768], P('section'), may hold values from -3 to 3
- gain_ffn: float32 [2, 768], P('section'), may hold values from 0.5 to 1.5
- shift_ffn: float32 [2, 768], P('section'), may hold values from -3 to 3
Outputs:
- activations: bfloat16 [2, 32768, 768], P('section', 'dp')
- input_grads: bfloat16 [2, 32768, 768], P('section', 'dp')
- grad_w_qkv: float32 [2, 768, 2304], P('section', 'dp')
- grad_w_out: float32 [2, 768, 768], P('section', 'dp')
- grad_gain_attn: float32 [2, 768], P('section', 'dp')
- grad_shift_attn: float32 [2, 768], P('section', 'dp')
- grad_w_up: float32 [2, 768, 3072], P('section', 'dp')
- grad_bias_up: float32 [2, 3072], P('section', 'dp')
- grad_w_down: float32 [2, 3072, 768], P('section', 'dp')
- grad_bias_down: float32 [2, 768], P('section', 'dp')
- grad_gain_ffn: float32 [2, 768], P('section', 'dp')
- grad_shift_ffn: float32 [2, 768], P('section', 'dp')
The draws below stay inside these ranges and needn't reach their ends.
All inputs are finite; a program needn't handle non-finite values.
Results may differ from the reference program's by a relative error of at most 0.02.
Values may be sent and summed in bfloat16 or wider, within the bound.
A program may use at most 512 MiB of HBM per device.

```python
import math
import jax
import jax.numpy as jnp
import numpy as np
from jax import lax

HEAD_DIM = 64
D = 768
FF = 3072
SEQ = 512
SEQS = 64
TOKENS = 32768
DOCS = 8
DOC_MOST = 128
FEATS = 128
FEAT_MOST = 8


def strengthened(values, stream_key, source, target, shards_of, factor):
    def block_of(axis_at):
        return (jnp.arange(values.shape[axis_at]) // (values.shape[axis_at] // shards_of)).reshape((-1,) + (1,) * (values.ndim - 1 - axis_at))

    first = jax.random.permutation(stream_key, shards_of)[block_of(target)]
    far = (block_of(target) + shards_of // 2) % shards_of
    return jnp.where((block_of(source) == first) | (block_of(source) == far), factor * values, values)


def steps_of(key, shape, pieces, smallest, high):
    loudness = 1.0
    for position, shards_of in pieces:
        heights = jax.random.uniform(jax.random.fold_in(jax.random.fold_in(key, 6), position), (shards_of,), jnp.float32, smallest / len(pieces), high / len(pieces))
        loudness = loudness * jnp.repeat(jnp.exp(heights), shape[position] // shards_of).reshape((-1,) + (1,) * (len(shape) - 1 - position))
    return loudness


def length_profile(number_of, total, most, slope):
    portions = [(1 << 20) // math.isqrt(rank ** slope) + 1 for rank in range(2, number_of + 1)]
    surplus, given = total - most - (number_of - 1), [1] * (number_of - 1)
    while surplus > 0:
        candidates = [i for i in range(number_of - 1) if given[i] < most]
        pool, left = sum([portions[i] for i in candidates]), surplus
        for i in candidates:
            addition = min(most - given[i], max(1, left * portions[i] // pool), surplus)
            given[i] = given[i] + addition
            surplus = surplus - addition
    return np.array([most] + given)


def ragged(rng, count, total, most, lean):
    if count == 2:
        one = jax.random.randint(rng, (), max(1, total - most), min(most, total - 1) + 1)
        return jnp.stack([one, total - one])
    sizes = jnp.asarray(length_profile(count, total, most, lean), jnp.int32)
    pairs = (count - 1) // 2
    donor, taker = sizes[1:1 + 2 * pairs:2], sizes[2:2 + 2 * pairs:2]
    slack = jnp.minimum(donor - 1, most - taker)
    passed = jax.random.randint(jax.random.fold_in(rng, 1), (pairs,), 0, 1 << 20) % (slack + 1)
    sizes = sizes.at[1:1 + 2 * pairs:2].set(donor - passed).at[2:2 + 2 * pairs:2].set(taker + passed)
    return sizes[jax.random.permutation(jax.random.fold_in(rng, 2), count)]


def bell_draw(own_key, extent, width, reach, split=(), held_as=jnp.bfloat16):
    values = width * jax.random.normal(own_key, extent, jnp.float32)
    if split:
        values = values * steps_of(own_key, extent, split, -0.22, 0.18)
    return jnp.clip(values, -reach, reach).astype(held_as)


def heavy_noise(stream_key, extent, width, most, pieces, heavy, held_as=jnp.bfloat16):
    drawn = width * jax.random.normal(stream_key, extent, jnp.float32)
    if pieces:
        drawn = drawn * steps_of(stream_key, extent, pieces, -0.22, 0.18)
    return jnp.clip(strengthened(drawn, jax.random.fold_in(stream_key, 3), *heavy), -most, most).astype(held_as)


def setup_inputs(seed: int = 0) -> dict:
    streams_of = jax.random.split(jax.random.key(seed), 15)
    return {
        "tokens": heavy_noise(streams_of[0], (TOKENS, D), 1.0, 6.0, ((0, 16),), (0, 1, 16, 2.0)),
        "cotangent": bell_draw(streams_of[1], (TOKENS, D), 1.0, 6.0, ((0, 16),)),
        "segment_ids": jax.vmap(lambda own: jnp.searchsorted(jnp.cumsum(ragged(own, DOCS, SEQ, DOC_MOST, 1)), jnp.arange(SEQ), side="right"))(jax.random.split(streams_of[2], SEQS)).reshape((SEQS, SEQ)).astype(jnp.int32),
        "feature_ids": jax.vmap(lambda own: jnp.searchsorted(jnp.cumsum(ragged(own, FEATS, SEQ, FEAT_MOST, 0)), jnp.arange(SEQ), side="right"))(jax.random.split(streams_of[3], SEQS)).reshape((SEQS, SEQ)).astype(jnp.int32),
        "w_qkv": bell_draw(streams_of[4], (2, D, 3 * D), D ** -0.5, 0.21875, ((0, 2),)),
        "w_out": bell_draw(streams_of[5], (2, D, D), (D // 16) ** -0.5, 0.875, ((0, 2),)),
        "gain_attn": jnp.clip(1.0 + 0.1 * jax.random.normal(streams_of[6], (2, D), jnp.float32), 0.5, 1.5),
        "shift_attn": bell_draw(streams_of[7], (2, D), 0.5, 3.0, ((0, 2),), jnp.float32),
        "w_up": bell_draw(streams_of[8], (2, D, FF), D ** -0.5, 0.21875, ((0, 2),)),
        "bias_up": bell_draw(streams_of[9], (2, FF), 0.5, 3.0, ((0, 2),), jnp.float32),
        "w_down": bell_draw(streams_of[10], (2, FF, D), FF ** -0.5, 0.109375, ((0, 2),)),
        "bias_down": bell_draw(streams_of[11], (2, D), 0.5, 3.0, ((0, 2),), jnp.float32),
        "gain_ffn": jnp.clip(1.0 + 0.1 * jax.random.normal(streams_of[12], (2, D), jnp.float32), 0.5, 1.5),
        "shift_ffn": bell_draw(streams_of[13], (2, D), 0.5, 3.0, ((0, 2),), jnp.float32),
    }


@jax.custom_vjp
def low(v):
    return lax.optimization_barrier(v.astype(jnp.bfloat16)).astype(jnp.float32)

@jax.custom_vjp
def low_back(v):
    return v

def low_keep(v):
    return (low(v), None)

def low_pass(kept, grad):
    return (grad,)

def back_keep(v):
    return (v, None)

def back_low(kept, grad):
    return (low(grad),)
low.defvjp(low_keep, low_pass)
low_back.defvjp(back_keep, back_low)
norm_eps = 1e-05
head_scale = 0.125
masked_score = -1e+30

def norm(values, gain_row, shift_row):
    centre = values - lax.optimization_barrier(jnp.mean(values, axis=-1, keepdims=True))
    inverse = lax.rsqrt(lax.optimization_barrier(jnp.mean(centre * centre, axis=-1, keepdims=True)) + norm_eps)
    return centre * inverse * gain_row + shift_row

def attend(queries, key_heads, value_heads, segments, groups):
    raw_scores = jnp.einsum('qhe,khe->hqk', queries, key_heads, precision=lax.Precision.HIGHEST) * head_scale
    scores = low_back(raw_scores)
    allowed = (segments[:, None] == segments[None, :]) & (groups[:, None] == groups[None, :])
    scores = jnp.where(allowed[None], scores, masked_score)
    prob_low = low(jax.nn.softmax(scores, axis=-1))
    return jnp.einsum('hqk,khe->qhe', prob_low, value_heads, precision=lax.Precision.HIGHEST)

def layer(weights, inputs, segments, groups):
    w_qkv, w_out, gain_attn, shift_attn, w_up, bias_up, w_down, bias_down, gain_ffn, shift_ffn = weights
    seq_count, seq_len = segments.shape
    model_width = inputs.shape[1]
    head_count = model_width // HEAD_DIM
    qkv_rows = jnp.dot(inputs, w_qkv, precision=lax.Precision.HIGHEST)

    def split_heads(columns):
        return low_back(low(columns)).reshape(seq_count, seq_len, head_count, HEAD_DIM)
    queries = split_heads(qkv_rows[:, :model_width])
    key_heads = split_heads(qkv_rows[:, model_width:2 * model_width])
    value_heads = split_heads(qkv_rows[:, 2 * model_width:])
    checked = jax.checkpoint(attend)
    context = lax.map(lambda sequence: checked(*sequence), (queries, key_heads, value_heads, segments, groups))
    context = low_back(low(context.reshape(-1, model_width)))
    attn_sum = inputs + low_back(jnp.dot(context, w_out, precision=lax.Precision.HIGHEST))
    normed = norm(attn_sum, gain_attn, shift_attn)
    pre_act = low_back(jnp.dot(low(normed), w_up, precision=lax.Precision.HIGHEST) + bias_up)
    activated = low(jax.nn.gelu(pre_act))
    ffn_sum = normed + low_back(jnp.dot(activated, w_down, precision=lax.Precision.HIGHEST) + bias_down)
    return norm(ffn_sum, gain_ffn, shift_ffn)

def reference(tokens, cotangent, segment_ids, feature_ids, w_qkv, w_out, gain_attn, shift_attn, w_up, bias_up, w_down, bias_down, gain_ffn, shift_ffn):
    stacked = tuple((weight.astype(jnp.float32) for weight in (w_qkv, w_out, gain_attn, shift_attn, w_up, bias_up, w_down, bias_down, gain_ffn, shift_ffn)))
    first = tuple((weight[0] for weight in stacked))
    second = tuple((weight[1] for weight in stacked))
    model_width = tokens.shape[1]
    block_count = segment_ids.shape[0] // 4
    inputs = tokens.reshape(block_count, 4 * SEQ, model_width)
    grads_in = cotangent.reshape(block_count, 4 * SEQ, model_width)
    segs = segment_ids.reshape(block_count, 4, SEQ)
    feats = feature_ids.reshape(block_count, 4, SEQ)

    def block_step(carry, block):
        block_in, block_grad, block_seg, block_feat = block
        hidden_out, back_first = jax.vjp(lambda params, values: layer(params, values, block_seg, block_feat), first, block_in.astype(jnp.float32))
        hidden_low = hidden_out.astype(jnp.bfloat16)
        final_out, back_second = jax.vjp(lambda params, values: layer(params, values, block_seg, jnp.zeros_like(block_feat)), second, hidden_low.astype(jnp.float32))
        grads_second, grad_hidden = back_second(block_grad.astype(jnp.float32))
        grad_low = grad_hidden.astype(jnp.bfloat16)
        grads_first, grad_tokens = back_first(grad_low.astype(jnp.float32))
        carry = tuple((running + jnp.stack([one_grad, two_grad]) for running, one_grad, two_grad in zip(carry, grads_first, grads_second)))
        return (carry, (hidden_low, final_out.astype(jnp.bfloat16), grad_tokens.astype(jnp.bfloat16), grad_low))
    init = tuple((jnp.zeros_like(weight) for weight in stacked))
    totals, (hidden_all, final_all, token_grads, hidden_grads) = lax.scan(block_step, init, (inputs, grads_in, segs, feats))
    activations = jnp.stack([hidden_all.reshape(-1, model_width), final_all.reshape(-1, model_width)])
    input_grads = jnp.stack([token_grads.reshape(-1, model_width), hidden_grads.reshape(-1, model_width)])
    return (activations, input_grads, totals[0], totals[1], totals[2], totals[3], totals[4], totals[5], totals[6], totals[7], totals[8], totals[9])
```

```python
import functools

import jax
import jax.numpy as jnp
from jax import lax
from jax.experimental import pallas as pl
from jax.experimental.pallas import tpu as pltpu
from jax.sharding import PartitionSpec as P_

BF, F32 = jnp.bfloat16, jnp.float32
SEQ, D, FF, QB, NQ, KW, PAIRS = 512, 768, 3072, 128, 4, 384, 6
EPS = 1e-5
C0, C1 = 0.7978845608028654, 0.044715
FC = 512


def dot(a,b): return lax.dot_general(a,b,(((1,),(0,)),((),())),preferred_element_type=F32)


def dnt(a,b): return lax.dot_general(a,b,(((1,),(1,)),((),())),preferred_element_type=F32)


def dtn(a,b): return lax.dot_general(a,b,(((0,),(0,)),((),())),preferred_element_type=F32)


def krange(qb):
    lo=max(0,(qb-1)*QB); hi=min(SEQ,(qb+2)*QB)
    return lo,hi


def norm_rows(v):
    c=v-jnp.mean(v,axis=-1,keepdims=True)
    r=lax.rsqrt(jnp.mean(c*c,axis=-1,keepdims=True)+EPS)
    return c*r, r


def make_bias(idc, idr, bias):
    for qb in range(NQ):
        lo,hi=krange(qb)
        same=idc[lo:hi,:]==idr[:,qb*QB:(qb+1)*QB]
        bias[qb,0:hi-lo,:]=jnp.where(same,0.0,-1e30).astype(F32)
VAR=2


def f_qkv(x, wqkv, qkv):
    qkv[:,0:D]=(dot(x[...],wqkv[:,0:D])*0.125).astype(BF)
    for j in range(1,3):
        qkv[:,j*D:(j+1)*D]=dot(x[...],wqkv[:,j*D:(j+1)*D]).astype(BF)


def head_masks(rows):
    lane=lax.broadcasted_iota(jnp.int32,(rows,128),1)
    return (lane<64)


def stack_heads(q, lo_b, hi_b):
    return jnp.concatenate([q*lo_b, q*hi_b],axis=0)


def lane_bf(w):
    lane=lax.broadcasted_iota(jnp.int32,(1,128),1)
    lo=jnp.where(lane<64,1.0,0.0).astype(BF); hi=jnp.where(lane<64,0.0,1.0).astype(BF)
    return lo,hi


def f_attn(qkv, bias, P, ctx):
    lo_b,hi_b=lane_bf(128)
    first=head_masks(QB)
    def pair_body(p0,_):
        items=[(pp,qb) for pp in range(2) for qb in range(NQ)]
        S={}
        def base_of(pp): return pl.multiple_of((p0*2+pp)*128,128)
        def qk(it):
            pp,qb=it; base=base_of(pp)
            lo,hi=krange(qb)
            q=qkv[qb*QB:(qb+1)*QB,pl.ds(base,128)]
            k=qkv[lo:hi,pl.ds(pl.multiple_of(D+base,128),128)]
            S[it]=dnt(k,stack_heads(q,lo_b,hi_b))
        def rest(it):
            pp,qb=it; base=base_of(pp); p=p0*2+pp
            lo,hi=krange(qb); kw=hi-lo
            s2=S.pop(it); b=bias[qb,0:kw,:]
            pn=[]
            for hd in range(2):
                s=s2[:,hd*QB:(hd+1)*QB]+b
                m=jnp.max(s,axis=0,keepdims=True)
                e=jnp.exp(s-m)
                t=jnp.sum(e,axis=0,keepdims=True)
                pb=(e*(1.0/t)).astype(BF)
                pn.append(pb)
            pb=jnp.concatenate(pn,axis=1)
            P[p,qb,0:kw,:]=pb
            v=qkv[lo:hi,pl.ds(pl.multiple_of(2*D+base,128),128)]
            o=dtn(pb,v)
            ctx[qb*QB:(qb+1)*QB,pl.ds(base,128)]=jnp.where(first,o[:QB],o[QB:]).astype(BF)
        for i,it in enumerate(items):
            if i<2: qk(it)
        for i,it in enumerate(items):
            if i+2<len(items): qk(items[i+2])
            rest(it)
        return 0
    lax.fori_loop(0,PAIRS//2,pair_body,0)


def f_mid(x, ctx, wout, ga, sa, n1, nl, r1, nf):
    RB=256
    for rb in range(SEQ//RB):
        rs=slice(rb*RB,(rb+1)*RB)
        a=x[rs,:].astype(F32)+dot(ctx[rs,:],wout[...])
        n,r=norm_rows(a)
        y=n*ga[...]+sa[...]
        n1[rs,:]=n.astype(BF); r1[rs,:]=jnp.broadcast_to(r,(RB,128))
        nl[rs,:]=y.astype(BF); nf[rs,:]=y


def gelu_both(p):
    p2=p*p
    t=jnp.tanh(p*(C0+(C0*C1)*p2))
    h=0.5+0.5*t
    d=h+ (p*(C0+(3*C0*C1)*p2))*(0.5-0.5*(t*t))
    return p*h, d


def f_ffn(nl, nf, wup, bu, wdown, bd, gf, sf, dg, act, n2, r2, h):
    NC=FF//FC
    for c in range(NC):
        cs=slice(c*FC,(c+1)*FC)
        p=dot(nl[...],wup[:,cs])+bu[:,cs]
        a,d=gelu_both(p)
        act[:,cs]=a.astype(BF); dg[:,cs]=d.astype(BF)
    RB=256
    for rb in range(SEQ//RB):
        rs=slice(rb*RB,(rb+1)*RB)
        f=nf[rs,:]+dot(act[rs,:],wdown[...])+bd[...]
        n,r=norm_rows(f)
        n2[rs,:]=n.astype(BF); r2[rs,:]=jnp.broadcast_to(r,(RB,128))
        h[rs,:]=(n*gf[...]+sf[...]).astype(BF)


def nb(e, n, r):
    return r*(e-jnp.mean(e,axis=-1,keepdims=True)-n*jnp.mean(e*n,axis=-1,keepdims=True))


def colsum8(v):
    R=v.shape[0]
    return jnp.sum(v.reshape(R//8,8,v.shape[1]),axis=0)


def b_ffn(g, n2, r2, gf, wdown, dg, wup, n1, r1, ga, down_in, up_in, dff, datt, out_in, sm, sbu):
    RB=256
    for rb in range(SEQ//RB):
        rs=slice(rb*RB,(rb+1)*RB)
        gg=g[rs,:].astype(F32); n=n2[rs,:].astype(F32); r=r2[rs,0:1]
        d=nb(gg*gf[...],n,r)
        dl=d.astype(BF)
        down_in[rs,:]=dl; dff[rs,:]=d
        sm[3]+=colsum8(gg*n); sm[4]+=colsum8(gg); sm[2]+=colsum8(dl.astype(F32))
    for c in range(FF//FC):
        cs=slice(c*FC,(c+1)*FC)
        u=(dnt(down_in[...],wdown[cs,:])*dg[:,cs].astype(F32)).astype(BF)
        up_in[:,cs]=u
        sbu[:,cs]+=colsum8(u.astype(F32))
    for rb in range(SEQ//RB):
        rs=slice(rb*RB,(rb+1)*RB)
        gg=dff[rs,:]+dnt(up_in[rs,:],wup[...])
        n=n1[rs,:].astype(F32); r=r1[rs,0:1]
        d=nb(gg*ga[...],n,r)
        datt[rs,:]=d; out_in[rs,:]=d.astype(BF)
        sm[0]+=colsum8(gg*n); sm[1]+=colsum8(gg)


def b_attn(out_in, wout, qkv, P, ctx, dctx, dq, dlt, vacc):
    dctx[...]=dnt(out_in[...],wout[...]).astype(BF)
    lo_b,hi_b=lane_bf(128)
    first=head_masks(QB)
    row=lax.broadcasted_iota(jnp.int32,(8,128),0); lane=lax.broadcasted_iota(jnp.int32,(8,128),1)
    sel=jnp.where((lane//64)==row,1.0,0.0).astype(BF)
    def pair(p,_):
        base=pl.multiple_of(p*128,128); kb=pl.multiple_of(D+base,128); vb=pl.multiple_of(2*D+base,128)
        dof=(dctx[:,pl.ds(base,128)].astype(F32)*ctx[:,pl.ds(base,128)].astype(F32)).astype(BF)
        dl=dnt(sel,dof)
        kparts={}; vparts={}
        for qb in range(NQ):
            lo,hi=krange(qb); kw=hi-lo
            qs=slice(qb*QB,(qb+1)*QB)
            q2=stack_heads(qkv[qs,pl.ds(base,128)],lo_b,hi_b)
            v=qkv[lo:hi,pl.ds(vb,128)]
            do2=stack_heads(dctx[qs,pl.ds(base,128)],lo_b,hi_b)
            dp=dnt(v,do2)
            pn=P[p,qb,0:kw,:]
            ds=[]
            for hd in range(2):
                hs=slice(hd*QB,(hd+1)*QB)
                ds.append((pn[:,hs].astype(F32)*(dp[:,hs]-dl[hd:hd+1,qs])).astype(BF))
            ds=jnp.concatenate(ds,axis=1)
            k=qkv[lo:hi,pl.ds(kb,128)]
            dqq=dtn(ds,k)
            dq[qs,pl.ds(base,128)]=(jnp.where(first,dqq[:QB],dqq[QB:])*0.125).astype(BF)
            dk=dot(ds,q2); dv=dot(pn,do2)
            for b in range(lo//QB,hi//QB):
                sl=slice(b*QB-lo,(b+1)*QB-lo)
                kparts[b]=dk[sl] if b not in kparts else kparts[b]+dk[sl]
                vparts[b]=dv[sl] if b not in vparts else vparts[b]+dv[sl]
            if qb>=1:
                b=qb-1
                dq[b*QB:(b+1)*QB,pl.ds(kb,128)]=kparts.pop(b).astype(BF); dq[b*QB:(b+1)*QB,pl.ds(vb,128)]=vparts.pop(b).astype(BF)
        b=NQ-1
        dq[b*QB:(b+1)*QB,pl.ds(kb,128)]=kparts.pop(b).astype(BF); dq[b*QB:(b+1)*QB,pl.ds(vb,128)]=vparts.pop(b).astype(BF)
        return 0
    lax.fori_loop(0,PAIRS,pair,0)
PSH=(6,4,384,256)
BSH=(4,384,128)


def b_in(dq, wqkv, datt, din):
    RB=256
    for rb in range(SEQ//RB):
        rs=slice(rb*RB,(rb+1)*RB)
        din[rs,:]=(datt[rs,:]+dnt(dq[rs,:],wqkv[...])).astype(BF)


SAVED = ("qkv", "P", "ctx", "n1", "r1", "nl", "dg", "act", "n2", "r2")
RELOADED = ("qkv", "P", "ctx", "n1", "r1", "dg", "n2", "r2")
ROWS = ("down_in", "up_in", "out_in", "dq")
SHAPES = dict(
    qkv=((SEQ, 3 * D), BF), P=((PAIRS, NQ, KW, 2 * QB), BF), ctx=((SEQ, D), BF), n1=((SEQ, D), BF), r1=((SEQ, 128), F32),
    nl=((SEQ, D), BF), dg=((SEQ, FF), BF), act=((SEQ, FF), BF), n2=((SEQ, D), BF), r2=((SEQ, 128), F32),
    down_in=((SEQ, D), BF), up_in=((SEQ, FF), BF), out_in=((SEQ, D), BF), dq=((SEQ, 3 * D), BF),
)
IN_NAMES = ("tokens", "cot", "idc", "idr", "wqkv_h", "wout_h", "wup_h", "wdown_h", "ga", "sa", "bu", "bd", "gf", "sf")
OUT_NAMES = ("h_all", "din_all", "sm", "sbu", "x_all") + tuple("s_" + k for k in SAVED) + tuple("s_" + k for k in ROWS)
SCRATCH = dict(
    io=((8, SEQ, D), BF), wqkv=((D, 3 * D), BF), wout=((D, D), BF), wup=((D, FF), BF), wdown=((FF, D), BF),
    nf=((SEQ, D), F32), datt=((SEQ, D), F32), dctx=((SEQ, D), BF), ho=((SEQ, D), BF), din=((SEQ, D), BF),
    bias=((NQ, KW, QB), F32), **SHAPES,
)


def pipeline_kernel(micro, *refs):
    names = IN_NAMES + OUT_NAMES + tuple(SCRATCH) + ("sem_w", "sem_own", "sem_f", "sem_l", "sem_b", "sem_x", "sem_ho", "sem_din", "send_h", "send_d", "recv")
    r = dict(zip(names, refs))
    sec = lax.axis_index("section")
    dp = lax.axis_index("dp")
    first_sec = sec == 0
    partner = (1 - sec, dp)
    barrier = pltpu.get_barrier_semaphore()
    pl.semaphore_signal(barrier, inc=1, device_id=partner, device_id_type=pl.DeviceIdType.MESH)

    def own_copy(src):
        return pltpu.make_async_copy(src, r["io"].at[pl.ds(0, micro)], r["sem_own"])

    weights = ("wqkv", "wout", "wup", "wdown")
    w_copies = [pltpu.make_async_copy(r[k + "_h"], r[k], r["sem_w"].at[i]) for i, k in enumerate(weights)]

    @pl.when(first_sec)
    def _():
        own_copy(r["tokens"]).start()

    @pl.when(jnp.logical_not(first_sec))
    def _():
        own_copy(r["cot"]).start()

    for c in w_copies:
        c.start()
    r["sm"][...] = jnp.zeros_like(r["sm"])
    r["sbu"][...] = jnp.zeros_like(r["sbu"])
    own_copy(r["tokens"]).wait()
    for c in w_copies:
        c.wait()
    pl.semaphore_wait(barrier, 1)

    def save(k, mb):
        return pltpu.make_async_copy(r[k], r["s_" + k].at[mb], r["sem_f"].at[SAVED.index(k)])

    def load(k, mb):
        return pltpu.make_async_copy(r["s_" + k].at[mb], r[k], r["sem_l"].at[RELOADED.index(k)])

    def save_rows(k, mb):
        return pltpu.make_async_copy(r[k], r["s_" + k].at[mb], r["sem_b"].at[ROWS.index(k)])

    def save_x(mb):
        return pltpu.make_async_copy(r["io"].at[mb + micro * sec], r["x_all"].at[mb], r["sem_x"])

    def save_h(mb):
        return pltpu.make_async_copy(r["ho"], r["h_all"].at[mb], r["sem_ho"])

    def save_din(mb):
        return pltpu.make_async_copy(r["din"], r["din_all"].at[mb], r["sem_din"])

    def send(k, mb, sem):
        return pltpu.make_async_remote_copy(
            src_ref=r[k], dst_ref=r["io"].at[micro + mb], send_sem=r[sem], recv_sem=r["recv"].at[mb],
            device_id=partner, device_id_type=pl.DeviceIdType.MESH,
        )

    EARLY_BOTH, EARLY_ONE = ("ctx", "nl"), ("qkv", "P", "n1", "r1")
    LATE_BOTH, LATE_ONE = ("act",), ("dg", "n2", "r2")

    def step(t, carry):
        is_f = jnp.where(first_sec, t < micro, lax.rem(t, 2) == 0)
        mb = jnp.where(first_sec, lax.rem(t, micro), lax.div(t, 2))
        after_f = jnp.where(first_sec, (t >= 1) & (t <= micro), lax.rem(t, 2) == 1)
        prev = jnp.where(first_sec, lax.rem(t + micro - 1, micro), lax.div(t, 2))

        def wait_late():
            for k in LATE_BOTH:
                save(k, prev).wait()
            save_h(prev).wait()

            @pl.when(first_sec)
            def _():
                for k in LATE_ONE:
                    save(k, prev).wait()
                send("ho", prev, "send_h").wait_send()

        @pl.when(after_f)
        def _():
            for k in EARLY_BOTH:
                save(k, prev).wait()
            save_x(prev).wait()

            @pl.when(first_sec)
            def _():
                for k in EARLY_ONE:
                    save(k, prev).wait()

        @pl.when(is_f)
        def _():
            rows = pl.ds(pl.multiple_of(mb * SEQ, SEQ), SEQ)
            make_bias(r["idc"].at[rows], r["idr"].at[mb], r["bias"])

            @pl.when(jnp.logical_not(first_sec))
            def _():
                send("ho", mb, "send_h").wait_recv()

            save_x(mb).start()
            x = r["io"].at[mb + micro * sec]
            f_qkv(x, r["wqkv"], r["qkv"])

            @pl.when(first_sec)
            def _():
                save("qkv", mb).start()

            f_attn(r["qkv"], r["bias"], r["P"], r["ctx"])
            save("ctx", mb).start()

            @pl.when(first_sec)
            def _():
                save("P", mb).start()

            f_mid(x, r["ctx"], r["wout"], r["ga"], r["sa"], r["n1"], r["nl"], r["r1"], r["nf"])
            save("nl", mb).start()

            @pl.when(first_sec)
            def _():
                save("n1", mb).start()
                save("r1", mb).start()

            @pl.when(after_f)
            def _():
                wait_late()

            f_ffn(r["nl"], r["nf"], r["wup"], r["bu"], r["wdown"], r["bd"], r["gf"], r["sf"], r["dg"], r["act"], r["n2"], r["r2"], r["ho"])
            save("act", mb).start()
            save_h(mb).start()

            @pl.when(first_sec)
            def _():
                send("ho", mb, "send_h").start()
                for k in LATE_ONE:
                    save(k, mb).start()

        @pl.when(jnp.logical_not(is_f))
        def _():
            @pl.when(first_sec)
            def _():
                @pl.when(after_f)
                def _():
                    wait_late()
                    for k in RELOADED:
                        load(k, mb).start()

                send("din", mb, "send_d").wait_recv()
                for k in RELOADED:
                    load(k, mb).wait()

            not_first_b = jnp.where(first_sec, t > micro, t > 1)
            before = mb - 1

            @pl.when(not_first_b)
            def _():
                for k in ROWS:
                    save_rows(k, before).wait()
                save_din(before).wait()

                @pl.when(jnp.logical_not(first_sec))
                def _():
                    send("din", before, "send_d").wait_send()

            g = r["io"].at[mb + micro * (1 - sec)]
            b_ffn(g, r["n2"], r["r2"], r["gf"], r["wdown"], r["dg"], r["wup"], r["n1"], r["r1"], r["ga"], r["down_in"], r["up_in"], r["nf"], r["datt"], r["out_in"], r["sm"], r["sbu"])
            for k in ROWS[:3]:
                save_rows(k, mb).start()

            @pl.when(jnp.logical_not(first_sec))
            def _():
                wait_late()

            b_attn(r["out_in"], r["wout"], r["qkv"], r["P"], r["ctx"], r["dctx"], r["dq"], None, None)
            save_rows("dq", mb).start()
            b_in(r["dq"], r["wqkv"], r["datt"], r["din"])
            save_din(mb).start()

            @pl.when(jnp.logical_not(first_sec))
            def _():
                send("din", mb, "send_d").start()

            @pl.when(first_sec & (mb < micro - 1))
            def _():
                for k in RELOADED:
                    load(k, mb + 1).start()

        return carry

    lax.fori_loop(0, 2 * micro, step, 0)
    last = micro - 1
    for k in ROWS:
        save_rows(k, last).wait()
    save_din(last).wait()

    @pl.when(jnp.logical_not(first_sec))
    def _():
        send("din", last, "send_d").wait_send()


def run_pipeline(tokens, cot, comb, weights, micro):
    w_qkv, w_out, gain_attn, shift_attn, w_up, bias_up, w_down, bias_down, gain_ffn, shift_ffn = weights
    any_space, vmem = pl.BlockSpec(memory_space=pl.ANY), pl.BlockSpec(memory_space=pltpu.VMEM)
    operands = (
        tokens.reshape(micro, SEQ, D), cot.reshape(micro, SEQ, D), comb.reshape(micro * SEQ, 1), comb.reshape(micro, 1, SEQ),
        w_qkv, w_out, w_up, w_down, gain_attn, shift_attn, bias_up, bias_down, gain_ffn, shift_ffn,
    )
    in_specs = [any_space] * 2 + [vmem] * 2 + [any_space] * 4 + [vmem] * 6
    out_shape = [
        jax.ShapeDtypeStruct((micro, SEQ, D), BF), jax.ShapeDtypeStruct((micro, SEQ, D), BF),
        jax.ShapeDtypeStruct((5, 8, D), F32), jax.ShapeDtypeStruct((8, FF), F32), jax.ShapeDtypeStruct((micro, SEQ, D), BF),
    ] + [jax.ShapeDtypeStruct((micro,) + SHAPES[k][0], SHAPES[k][1]) for k in SAVED + ROWS]
    out_specs = [any_space] * 2 + [vmem] * 2 + [any_space] * (len(out_shape) - 4)
    dma = pltpu.SemaphoreType.DMA
    scratch = [pltpu.VMEM(*SCRATCH[k]) for k in SCRATCH] + [
        dma((4,)), dma, dma((len(SAVED),)), dma((len(RELOADED),)), dma((len(ROWS),)), dma, dma, dma, dma, dma, dma((micro,)),
    ]
    outs = pl.pallas_call(
        functools.partial(pipeline_kernel, micro), out_shape=out_shape, in_specs=in_specs, out_specs=out_specs, scratch_shapes=scratch,
        name="pipeline",
        compiler_params=pltpu.CompilerParams(collective_id=1, has_side_effects=True, vmem_limit_bytes=62 * 2**20),
    )(*operands)
    return dict(zip(OUT_NAMES, outs))


def weight_product(left, right):
    rows = left.shape[0] * left.shape[1]
    return lax.dot_general(
        left.reshape(rows, -1), right.reshape(rows, -1), (((0,), (0,)), ((), ())), preferred_element_type=F32
    )


def body(
    tokens, cotangent, segment_ids, feature_ids, w_qkv, w_out, gain_attn, shift_attn, w_up, bias_up, w_down, bias_down, gain_ffn, shift_ffn
):
    sec = lax.axis_index("section")
    micro = segment_ids.shape[0]
    comb = segment_ids * 128 + feature_ids * (1 - sec)
    weights = (w_qkv[0], w_out[0], gain_attn, shift_attn, w_up[0], bias_up, w_down[0], bias_down, gain_ffn, shift_ffn)
    o = run_pipeline(tokens, cotangent, comb, weights, micro)
    sm = jnp.sum(o["sm"], axis=1)
    sbu = jnp.sum(o["sbu"], axis=0)
    scatter = lambda v: lax.psum_scatter(v, "dp", scatter_dimension=0, tiled=True)[None]
    g_qkv = scatter(weight_product(o["x_all"], o["s_dq"]))
    g_out = scatter(weight_product(o["s_ctx"], o["s_out_in"]))
    g_up = scatter(weight_product(o["s_nl"], o["s_up_in"]))
    g_down = scatter(weight_product(o["s_act"], o["s_down_in"]))
    return (
        o["h_all"].reshape(1, micro * SEQ, D), o["din_all"].reshape(1, micro * SEQ, D), g_qkv, g_out, scatter(sm[0]), scatter(sm[1]),
        g_up, scatter(sbu), g_down, scatter(sm[2]), scatter(sm[3]), scatter(sm[4]),
    )


def solution(mesh):
    rows, mat, vec = P_("dp", None), P_("section", None, None), P_("section", None)
    in_specs = (rows,) * 4 + (mat, mat, vec, vec, mat, vec, mat, vec, vec, vec)
    big, small = P_("section", "dp", None), P_("section", "dp")
    out_specs = (big, big, big, big, small, small, big, small, big, small, small, small)
    return jax.shard_map(body, mesh=mesh, in_specs=in_specs, out_specs=out_specs, check_vma=False)
```

```python
import functools
import types

import jax
import jax.numpy as jnp
from jax import lax
from jax.experimental import pallas as pl
from jax.experimental.pallas import tpu as pltpu
from jax.sharding import PartitionSpec

BF, F32 = jnp.bfloat16, jnp.float32
SEQ, D, FF, HEAD = 512, 768, 3072, 64
QB, NQ, KW = 128, 4, 384
QUADS, QW = 3, 256
FC, RB = 512, 256
EPS = 1e-5
C0, C1 = 0.7978845608028654, 0.044715
MESH = pl.DeviceIdType.MESH


def dot(a, b):
    return lax.dot_general(a, b, (((1,), (0,)), ((), ())), preferred_element_type=F32)


def dot_nt(a, b):
    return lax.dot_general(a, b, (((1,), (1,)), ((), ())), preferred_element_type=F32)


def dot_tn(a, b):
    return lax.dot_general(a, b, (((0,), (0,)), ((), ())), preferred_element_type=F32)


def keys_of(block, reach):
    return max(0, block * QB - reach), min(SEQ, (block + 1) * QB + reach)


REACH = (16, 128)


def row_blocks(size=RB):
    return [slice(n * size, (n + 1) * size) for n in range(SEQ // size)]


def norm_rows(v):
    c = v - jnp.mean(v, axis=-1, keepdims=True)
    r = lax.rsqrt(jnp.mean(c * c, axis=-1, keepdims=True) + EPS)
    return c * r, r


def norm_back(e, n, r):
    return r * (e - jnp.mean(e, axis=-1, keepdims=True) - n * jnp.mean(e * n, axis=-1, keepdims=True))


def column_sums(v):
    return jnp.sum(v.reshape(v.shape[0] // 8, 8, v.shape[1]), axis=0)


def make_bias(id_col, id_row, bias, reach):
    for qb in range(NQ):
        lo, hi = keys_of(qb, reach)
        same = id_col[lo:hi, :] == id_row[:, qb * QB:(qb + 1) * QB]
        bias[qb, 0:hi - lo, :] = jnp.where(same, 0.0, -1e30).astype(F32)


def head_lanes():
    lane = lax.broadcasted_iota(jnp.int32, (1, QW), 1)
    return [jnp.where((lane >= HEAD * i) & (lane < HEAD * (i + 1)), 1.0, 0.0).astype(BF) for i in range(4)]


def by_head(v, masks):
    return jnp.concatenate([v * m for m in masks], axis=0)


def f_qkv(x, w_qkv, qkv):
    qkv[:, 0:D] = (dot(x[...], w_qkv[:, 0:D]) * 0.125).astype(BF)
    for j in range(1, 3):
        qkv[:, j * D:(j + 1) * D] = dot(x[...], w_qkv[:, j * D:(j + 1) * D]).astype(BF)


def f_attention(qkv, bias, probs, ctx, inv, reach):
    first = lax.broadcasted_iota(jnp.int32, (QB, 128), 1) < HEAD
    masks = head_lanes()
    ones = jnp.ones((KW, 128), BF)

    def quad(p, carry):
        base = pl.multiple_of(p * QW, QW)
        scores = {}

        def begin(qb):
            lo, hi = keys_of(qb, reach)
            q = qkv[qb * QB:(qb + 1) * QB, pl.ds(base, QW)]
            k = qkv[lo:hi, pl.ds(pl.multiple_of(D + base, QW), QW)]
            scores[qb] = dot_nt(k, by_head(q, masks))

        def finish(qb):
            lo, hi = keys_of(qb, reach)
            kw, qs = hi - lo, slice(qb * QB, (qb + 1) * QB)
            v = qkv[lo:hi, pl.ds(pl.multiple_of(2 * D + base, QW), QW)]
            all_four, b, e = scores.pop(qb), bias[qb, 0:kw, :], []
            for hd in range(4):
                s = all_four[:, hd * QB:(hd + 1) * QB] + b
                e.append(jnp.exp((s - jnp.max(s, axis=0, keepdims=True)).astype(BF)))
                probs[p, qb, 0:kw, hd * QB:(hd + 1) * QB] = e[hd]
            for n in range(2):
                right = jnp.concatenate([v[:, n * 128:(n + 1) * 128], ones[:kw]], axis=1)
                o = dot_tn(jnp.concatenate(e[2 * n:2 * n + 2], axis=1), right)
                value = jnp.where(first, o[:QB, :128], o[QB:, :128])
                recip = 1.0 / jnp.where(first, o[:QB, 128:], o[QB:, 128:])
                inv[qs, pl.ds(base + n * 128, 128)] = recip
                ctx[qs, pl.ds(base + n * 128, 128)] = (value * recip).astype(BF)

        begin(0)
        begin(1)
        for qb in range(NQ):
            if qb + 2 < NQ:
                begin(qb + 2)
            finish(qb)
        return carry

    lax.fori_loop(0, QUADS, quad, 0)


def f_mid(x, ctx, w_out, gain, shift, n1, nl, r1, nf):
    for rs in row_blocks():
        n, r = norm_rows(x[rs, :].astype(F32) + dot(ctx[rs, :], w_out[...]))
        out = n * gain[...] + shift[...]
        n1[rs, :] = n.astype(BF)
        r1[rs, :] = jnp.broadcast_to(r, (RB, 128))
        nl[rs, :] = out.astype(BF)
        nf[rs, :] = out


def gelu_both(p):
    p2 = p * p
    t = jnp.tanh(p * (C0 + (C0 * C1) * p2))
    h = 0.5 + 0.5 * t
    return p * h, h + (p * (C0 + (3 * C0 * C1) * p2)) * (0.5 - 0.5 * (t * t))


def f_ffn(nl, nf, w_up, b_up, w_down, b_down, gain, shift, dg, act, n2, r2, h):
    for c in range(FF // FC):
        cs = slice(c * FC, (c + 1) * FC)
        a, d = gelu_both(dot(nl[...], w_up[:, cs]) + b_up[:, cs])
        act[:, cs] = a.astype(BF)
        dg[:, cs] = d.astype(BF)
    for rs in row_blocks():
        n, r = norm_rows(nf[rs, :] + dot(act[rs, :], w_down[...]) + b_down[...])
        n2[rs, :] = n.astype(BF)
        r2[rs, :] = jnp.broadcast_to(r, (RB, 128))
        h[rs, :] = (n * gain[...] + shift[...]).astype(BF)


def b_ffn(g, n2, r2, gain_ffn, w_down, dg, w_up, n1, r1, gain_attn, down_in, up_in, d_ffn, d_attn, out_in, sm, sbu):
    for rs in row_blocks():
        grad, n, r = g[rs, :].astype(F32), n2[rs, :].astype(F32), r2[rs, 0:1]
        d = norm_back(grad * gain_ffn[...], n, r)
        low = d.astype(BF)
        down_in[rs, :] = low
        d_ffn[rs, :] = d
        sm[3] += column_sums(grad * n)
        sm[4] += column_sums(grad)
        sm[2] += column_sums(low.astype(F32))
    for c in range(FF // FC):
        cs = slice(c * FC, (c + 1) * FC)
        u = (dot_nt(down_in[...], w_down[cs, :]) * dg[:, cs].astype(F32)).astype(BF)
        up_in[:, cs] = u
        sbu[:, cs] += column_sums(u.astype(F32))
    for rs in row_blocks():
        grad = d_ffn[rs, :] + dot_nt(up_in[rs, :], w_up[...])
        n, r = n1[rs, :].astype(F32), r1[rs, 0:1]
        d = norm_back(grad * gain_attn[...], n, r)
        d_attn[rs, :] = d
        out_in[rs, :] = d.astype(BF)
        sm[0] += column_sums(grad * n)
        sm[1] += column_sums(grad)


def b_attention(qkv, probs, ctx, d_ctx, d_qkv, reach):
    first = lax.broadcasted_iota(jnp.int32, (QB, 128), 1) < HEAD
    masks = head_lanes()
    pick = jnp.where(lax.broadcasted_iota(jnp.int32, (8, QW), 1) // HEAD == lax.broadcasted_iota(jnp.int32, (8, QW), 0), 1.0, 0.0).astype(BF)
    edges = sorted({e for qb in range(NQ) for e in keys_of(qb, reach)})

    def quad(p, carry):
        base = pl.multiple_of(p * QW, QW)
        kb, vb = pl.multiple_of(D + base, QW), pl.multiple_of(2 * D + base, QW)
        both = (d_ctx[:, pl.ds(base, QW)].astype(F32) * ctx[:, pl.ds(base, QW)].astype(F32)).astype(BF)
        delta = dot_nt(pick, both)
        d_prob, d_k, d_v = {}, {}, {}

        def begin(qb):
            lo, hi = keys_of(qb, reach)
            do = d_ctx[qb * QB:(qb + 1) * QB, pl.ds(base, QW)]
            d_prob[qb] = dot_nt(qkv[lo:hi, pl.ds(vb, QW)], by_head(do, masks))

        def finish(qb):
            lo, hi = keys_of(qb, reach)
            kw, qs = hi - lo, slice(qb * QB, (qb + 1) * QB)
            all_four, e, ds = d_prob.pop(qb), probs[p, qb, 0:kw, :], []
            for hd in range(4):
                hs = slice(hd * QB, (hd + 1) * QB)
                ds.append((e[:, hs].astype(F32) * (all_four[:, hs] - delta[hd:hd + 1, qs])).astype(BF))
            ds = jnp.concatenate(ds, axis=1)
            d_v[qb] = dot(e, by_head(d_ctx[qs, pl.ds(base, QW)], masks))
            d_k[qb] = dot(ds, by_head(qkv[qs, pl.ds(base, QW)], masks))
            k = qkv[lo:hi, pl.ds(kb, QW)]
            for n in range(2):
                o = dot_tn(ds[:, n * 2 * QB:(n + 1) * 2 * QB], k[:, n * 128:(n + 1) * 128])
                d_qkv[qs, pl.ds(base + n * 128, 128)] = (jnp.where(first, o[:QB], o[QB:]) * 0.125).astype(BF)

        def flush(done):
            low = keys_of(done, reach)[0]
            high = keys_of(done + 1, reach)[0] if done + 1 < NQ else SEQ
            for a, b in zip(edges, edges[1:]):
                if low <= a and b <= high:
                    for parts, col in ((d_k, kb), (d_v, vb)):
                        pieces = [parts[n][a - keys_of(n, reach)[0]:b - keys_of(n, reach)[0]] for n in parts if keys_of(n, reach)[0] <= a and b <= keys_of(n, reach)[1]]
                        d_qkv[a:b, pl.ds(col, QW)] = functools.reduce(lambda v, w: v + w, pieces).astype(BF)

        begin(0)
        begin(1)
        for qb in range(NQ):
            if qb + 2 < NQ:
                begin(qb + 2)
            finish(qb)
            flush(qb)
        return carry

    lax.fori_loop(0, QUADS, quad, 0)


def b_input(d_qkv, w_qkv, d_attn, d_in):
    for rs in row_blocks():
        d_in[rs, :] = (d_attn[rs, :] + dot_nt(d_qkv[rs, :], w_qkv[...])).astype(BF)


def arrays(**named):
    return named


SAVED = arrays(
    qkv=((SEQ, 3 * D), BF), probs=((QUADS, NQ, KW, 4 * QB), BF), ctx=((SEQ, D), BF), inv=((SEQ, D), F32), n1=((SEQ, D), BF), r1=((SEQ, 128), F32),
    nl=((SEQ, D), BF), dg=((SEQ, FF), BF), act=((SEQ, FF), BF), n2=((SEQ, D), BF), r2=((SEQ, 128), F32),
)
ROWS = arrays(down_in=((SEQ, D), BF), up_in=((SEQ, FF), BF), out_in=((SEQ, D), BF), dq=((SEQ, 3 * D), BF))
EARLY_BOTH, EARLY_ONE = tuple(arrays(ctx=0, nl=0)), tuple(arrays(qkv=0, probs=0, inv=0, n1=0, r1=0))
LATE_ONE = tuple(arrays(dg=0, n2=0, r2=0))
RELOADED = tuple(k for k in SAVED if k not in tuple(arrays(nl=0, act=0)))
WEIGHTS = arrays(wqkv=((D, 3 * D), BF), wout=((D, D), BF), wup=((D, FF), BF), wdown=((FF, D), BF))
INPUTS = arrays(tokens=0, cot=0, id_col=0, id_row=0, ga=0, sa=0, bu=0, bd=0, gf=0, sf=0)
SCRATCH = arrays(
    io=((8, SEQ, D), BF), nf=((SEQ, D), F32), datt=((SEQ, D), F32), dctx=((SEQ, D), BF), ho=((SEQ, D), BF), din=((SEQ, D), BF),
    bias=((4, NQ, KW, QB), F32), **WEIGHTS, **SAVED, **ROWS,
)
SEMS = arrays(s_w=(4,), s_own=(1,), s_f=(len(SAVED),), s_l=(len(SAVED),), s_b=(len(ROWS),), s_x=(1,), s_ho=(1,), s_din=(1,), s_sh=(1,), s_sd=(1,), s_r=(4,))


def pipeline_kernel(micro, *refs):
    n_in, n_w, n_out = len(INPUTS), len(WEIGHTS), 5 + len(SAVED) + len(ROWS)
    r = types.SimpleNamespace(**dict(zip(INPUTS, refs)))
    w_hbm = dict(zip(WEIGHTS, refs[n_in:]))
    h_all, din_all, sm, sbu, x_all = refs[n_in + n_w:][:5]
    kept = dict(zip((*SAVED, *ROWS), refs[n_in + n_w + 5:]))
    scratch = dict(zip((*SCRATCH, *SEMS), refs[n_in + n_w + n_out:]))
    s = types.SimpleNamespace(**scratch)
    sec, dp = lax.axis_index("section"), lax.axis_index("dp")
    core = lax.rem(dp, 2)
    first_sec = sec == 0
    second_sec = jnp.logical_not(first_sec)
    partner = (1 - sec, dp)
    barrier = pltpu.get_barrier_semaphore()
    pl.semaphore_signal(barrier, inc=1, device_id=partner, device_id_type=MESH)

    def own_copy(src):
        return pltpu.make_async_copy(src, s.io.at[pl.ds(0, micro)], s.s_own.at[0])

    w_copies = [pltpu.make_async_copy(w_hbm[k], scratch[k], s.s_w.at[n]) for n, k in enumerate(WEIGHTS)]

    @pl.when(first_sec)
    def _():
        own_copy(r.tokens).start()

    @pl.when(second_sec)
    def _():
        own_copy(r.cot).start()

    for c in w_copies:
        c.start()
    sm[...] = jnp.zeros_like(sm)
    sbu[...] = jnp.zeros_like(sbu)

    def bias_of(mb, reach):
        make_bias(r.id_col.at[pl.ds(pl.multiple_of(mb * SEQ, SEQ), SEQ)], r.id_row.at[mb], s.bias.at[mb], reach)

    @pl.when(first_sec)
    def _():
        bias_of(0, REACH[0])

    @pl.when(second_sec)
    def _():
        lax.fori_loop(0, micro, lambda mb, c: (bias_of(mb, REACH[1]), c)[1], 0)

    own_copy(r.tokens).wait()
    for c in w_copies:
        c.wait()
    pl.semaphore_wait(barrier, 1)

    order = tuple(SAVED)

    def save(k, mb):
        return pltpu.make_async_copy(scratch[k], kept[k].at[mb], s.s_f.at[order.index(k)])

    def load(k, mb):
        return pltpu.make_async_copy(kept[k].at[mb], scratch[k], s.s_l.at[order.index(k)])

    def save_rows(k, mb):
        return pltpu.make_async_copy(scratch[k], kept[k].at[mb], s.s_b.at[tuple(ROWS).index(k)])

    def save_x(mb):
        return pltpu.make_async_copy(s.io.at[mb + micro * sec], x_all.at[mb], s.s_x.at[0])

    def save_act(mb):
        return save(order[8], mb)

    def save_h(mb):
        return pltpu.make_async_copy(s.ho, h_all.at[mb], s.s_ho.at[0])

    def save_din(mb):
        return pltpu.make_async_copy(s.din, din_all.at[mb], s.s_din.at[0])

    def send(src, mb, sem):
        return pltpu.make_async_remote_copy(
            src_ref=src, dst_ref=s.io.at[micro + mb], send_sem=sem.at[0], recv_sem=s.s_r.at[mb], device_id=partner, device_id_type=MESH
        )

    def send_h(mb):
        return send(s.ho, mb, s.s_sh)

    def send_din(mb):
        return send(s.din, mb, s.s_sd)

    def step(t, carry):
        is_f = jnp.where(first_sec, t < micro, lax.rem(t, 2) == 0)
        mb = jnp.where(first_sec, lax.rem(t, micro), lax.div(t, 2))
        after_f = jnp.where(first_sec, (t >= 1) & (t <= micro), lax.rem(t, 2) == 1)
        prev = jnp.where(first_sec, lax.rem(t + micro - 1, micro), lax.div(t, 2))
        late_send = first_sec & (core == 1)

        def wait_late():
            save_act(prev).wait()
            save_h(prev).wait()

            @pl.when(first_sec)
            def _():
                for k in LATE_ONE:
                    save(k, prev).wait()
                send_h(prev).wait_send()

        @pl.when(after_f)
        def _():
            for k in EARLY_BOTH:
                save(k, prev).wait()
            save_x(prev).wait()

            @pl.when(first_sec)
            def _():
                for k in EARLY_ONE:
                    save(k, prev).wait()

        @pl.when(is_f)
        def _():
            @pl.when(second_sec)
            def _():
                send_h(mb).wait_recv()

            save_x(mb).start()
            x = s.io.at[mb + micro * sec]
            f_qkv(x, s.wqkv, s.qkv)

            @pl.when(first_sec)
            def _():
                save(order[0], mb).start()
                f_attention(s.qkv, s.bias.at[mb], s.probs, s.ctx, s.inv, REACH[0])
                for k in EARLY_ONE[1:3]:
                    save(k, mb).start()

            @pl.when(second_sec)
            def _():
                f_attention(s.qkv, s.bias.at[mb], s.probs, s.ctx, s.inv, REACH[1])

            @pl.when(late_send & (t == 1))
            def _():
                send_h(0).start()

            save(EARLY_BOTH[0], mb).start()
            f_mid(x, s.ctx, s.wout, r.ga, r.sa, s.n1, s.nl, s.r1, s.nf)
            save(EARLY_BOTH[1], mb).start()

            @pl.when(first_sec)
            def _():
                for k in EARLY_ONE[3:]:
                    save(k, mb).start()

            @pl.when(after_f)
            def _():
                wait_late()

            f_ffn(s.nl, s.nf, s.wup, r.bu, s.wdown, r.bd, r.gf, r.sf, s.dg, s.act, s.n2, s.r2, s.ho)

            @pl.when(first_sec & jnp.logical_not(late_send & (t == 0)))
            def _():
                send_h(mb).start()

            save_act(mb).start()
            save_h(mb).start()

            @pl.when(first_sec)
            def _():
                for k in LATE_ONE:
                    save(k, mb).start()

                @pl.when(t < micro - 1)
                def _():
                    bias_of(mb + 1, REACH[0])

        @pl.when(jnp.logical_not(is_f))
        def _():
            @pl.when(first_sec)
            def _():
                @pl.when(after_f)
                def _():
                    wait_late()
                    for k in RELOADED:
                        load(k, mb).start()

                for k in RELOADED:
                    load(k, mb).wait()
                send_din(mb).wait_recv()

            not_first_b = jnp.where(first_sec, t > micro, t > 1)
            before = mb - 1

            @pl.when(not_first_b)
            def _():
                for k in ROWS:
                    save_rows(k, before).wait()
                save_din(before).wait()

                @pl.when(second_sec)
                def _():
                    send_din(before).wait_send()

            g = s.io.at[mb + micro * (1 - sec)]
            b_ffn(g, s.n2, s.r2, r.gf, s.wdown, s.dg, s.wup, s.n1, s.r1, r.ga, s.down_in, s.up_in, s.nf, s.datt, s.out_in, sm, sbu)
            for k in tuple(ROWS)[:3]:
                save_rows(k, mb).start()

            @pl.when(second_sec)
            def _():
                wait_late()

            s.dctx[...] = (dot_nt(s.out_in[...], s.wout[...]) * s.inv[...]).astype(BF)

            @pl.when(first_sec)
            def _():
                b_attention(s.qkv, s.probs, s.ctx, s.dctx, s.dq, REACH[0])

            @pl.when(second_sec)
            def _():
                b_attention(s.qkv, s.probs, s.ctx, s.dctx, s.dq, REACH[1])

            save_rows(tuple(ROWS)[3], mb).start()
            b_input(s.dq, s.wqkv, s.datt, s.din)

            @pl.when(second_sec)
            def _():
                send_din(mb).start()

            save_din(mb).start()

            @pl.when(first_sec & (mb < micro - 1))
            def _():
                for k in RELOADED:
                    load(k, mb + 1).start()

        return carry

    lax.fori_loop(0, 2 * micro, step, 0)
    last = micro - 1
    for k in ROWS:
        save_rows(k, last).wait()
    save_din(last).wait()

    @pl.when(second_sec)
    def _():
        send_din(last).wait_send()


def run_pipeline(tokens, cot, comb, weights, micro):
    w_qkv, w_out, gain_attn, shift_attn, w_up, bias_up, w_down, bias_down, gain_ffn, shift_ffn = weights
    any_space, vmem = pl.BlockSpec(memory_space=pl.ANY), pl.BlockSpec(memory_space=pltpu.VMEM)
    operands = (
        tokens.reshape(micro, SEQ, D), cot.reshape(micro, SEQ, D), comb.reshape(micro * SEQ, 1), comb.reshape(micro, 1, SEQ),
        gain_attn, shift_attn, bias_up, bias_down, gain_ffn, shift_ffn, w_qkv, w_out, w_up, w_down,
    )
    in_specs = [any_space] * 2 + [vmem] * 8 + [any_space] * 4
    out_shape = [
        jax.ShapeDtypeStruct((micro, SEQ, D), BF), jax.ShapeDtypeStruct((micro, SEQ, D), BF),
        jax.ShapeDtypeStruct((5, 8, D), F32), jax.ShapeDtypeStruct((8, FF), F32), jax.ShapeDtypeStruct((micro, SEQ, D), BF),
    ] + [jax.ShapeDtypeStruct((micro,) + shape, dtype) for shape, dtype in (*SAVED.values(), *ROWS.values())]
    out_specs = [any_space] * 2 + [vmem] * 2 + [any_space] * (len(out_shape) - 4)
    scratch = [pltpu.VMEM(*v) for v in SCRATCH.values()] + [pltpu.SemaphoreType.DMA(v) for v in SEMS.values()]
    outs = pl.pallas_call(
        functools.partial(pipeline_kernel, micro), out_shape=out_shape, in_specs=in_specs, out_specs=out_specs, scratch_shapes=scratch,
        name="pipeline",
        compiler_params=pltpu.CompilerParams(collective_id=1, has_side_effects=True, vmem_limit_bytes=63 * 2**20),
    )(*operands)
    return outs[:4], types.SimpleNamespace(x_all=outs[4], **dict(zip((*SAVED, *ROWS), outs[5:])))


WAITS = (1, 3, 5, 6, 7)
Z_WAITS = (1, 3, 4, 6, 7)
Z_FIRST = (0, 1)
BLOCK, ROW_SET = 0, 1
ITEMS = ((BLOCK, 0), (ROW_SET, 3), (ROW_SET, 0), (BLOCK, 1), (ROW_SET, 2), (ROW_SET, 1)) + tuple((BLOCK, i) for i in range(2, 8))
W_IN = arrays(x_all=0, dq=0, ctx=0, out_in=0, nl=0, up_in=0, act=0, down_in=0, sm=0, sbu=0)
W_OUT = arrays(g_qkv=0, g_out=0, g_up=0, g_down=0, g_ga=0, g_sa=0, g_bu=0, g_bd=0, g_gf=0, g_sf=0)
NC = 8
W_SCRATCH = arrays(
    a_buf=((2, 4, SEQ, D), BF), b_buf=((2, 4, SEQ, D), BF), prod=((16, 48, D), F32),
    c_send=((NC, 4, 2, 48, D), BF), c_own=((NC, 4, 2, 48, D), BF), c_r0=((NC, 4, 2, 48, D), BF),
    c_r1=((NC, 4, 48, D), BF), c_u=((NC, 4, 48, D), BF), c_r2=((NC, 2, 4, 48, D), BF),
    d_send=((4, 2, 192, D), BF), d_own=((4, 2, 192, D), BF), d_r0=((4, 2, 192, D), BF),
    d_r1=((4, 192, D), BF), d_u=((4, 192, D), BF), d_r2=((2, 4, 192, D), BF),
    z_r2=((2, 2, 4, 2, 48, D), BF), z_v=((2, 48, D), BF), z_r4=((2, 48, D), BF),
    small=((5, 16, D), F32), small_r=((4, 16, D), F32),
)
W_SEMS = arrays(
    l_a=(2,), l_b=(2,), cs0=(NC,), cr0=(NC,), cs1=(NC,), cr1=(NC,), cs2=(NC, 2, 4), cr2=(NC, 2, 4),
    ds0=(4,), dr0=(4,), ds1=(4,), dr1=(4,), ds2=(2, 4), dr2=(2, 4), ss=(4,), sr=(4,), zs4=(2,), zr4=(2,),
)


def weights_kernel(*refs):
    r = types.SimpleNamespace(**dict(zip((*W_IN, *W_OUT, *W_SCRATCH, *W_SEMS), refs)))
    sec, dp = lax.axis_index("section"), lax.axis_index("dp")
    core, y, z = lax.rem(dp, 2), lax.rem(lax.div(dp, 2), 2), lax.div(dp, 4)
    oc, oy = 1 - core, 1 - y
    at = lambda c_, y_, z_: (sec, z_ * 4 + y_ * 2 + c_)
    to_core, to_y = at(oc, y, z), at(core, oy, z)
    to_z1, to_z2 = at(core, y, z + 1 - 2 * lax.rem(z, 2)), at(core, y, lax.rem(z + 2, 4))
    end_z, mid_z = (z == 0) | (z == 3), (z == 1) | (z == 2)
    barrier = pltpu.get_barrier_semaphore()
    for peer in (to_core, to_y, at(core, y, lax.rem(z + 1, 4)), to_z2, at(core, y, lax.rem(z + 3, 4))):
        pl.semaphore_signal(barrier, inc=1, device_id=peer, device_id_type=MESH)

    def send(src, dst, s, q, peer):
        return pltpu.make_async_remote_copy(src_ref=src, dst_ref=dst, send_sem=s, recv_sem=q, device_id=peer, device_id_type=MESH)

    def block(ref, j):
        return ref if ref.shape[2] == D else ref.at[:, :, pl.ds(j, D)]

    def operands(item):
        i = item[1]
        if item[0] == ROW_SET:
            return block(r.act, i * D), block(r.down_in, 0)
        if i < 3:
            return block(r.x_all, 0), block(r.dq, i * D)
        if i == 3:
            return block(r.ctx, 0), block(r.out_in, 0)
        return block(r.nl, 0), block(r.up_in, (i - 4) * D)

    def loads(n):
        a, b = operands(ITEMS[n])
        k = n % 2
        return pltpu.make_async_copy(a, r.a_buf.at[k], r.l_a.at[k]), pltpu.make_async_copy(b, r.b_buf.at[k], r.l_b.at[k])

    f = lambda v: v.astype(F32)
    def c0(i):
        return send(r.c_send.at[i], r.c_r0.at[i], r.cs0.at[i], r.cr0.at[i], to_core)

    def c1(i):
        return send(r.c_own.at[i, :, oy], r.c_r1.at[i], r.cs1.at[i], r.cr1.at[i], to_y)

    def c2(i, way, t):
        src, dst = (r.c_own, r.z_r2) if i in Z_FIRST else (r.c_u, r.c_r2)
        return send(src.at[i, t], dst.at[i, way, t], r.cs2.at[i, way, t], r.cr2.at[i, way, t], at(core, y, z + 1 - 2 * way))

    def z4(i):
        return send(r.z_v.at[i], r.z_r4.at[i], r.zs4.at[i], r.zr4.at[i], to_y)

    def c_target(i):
        if i < 3:
            return r.g_qkv.at[:, pl.ds(i * D, D)]
        return r.g_out if i == 3 else r.g_up.at[:, pl.ds((i - 4) * D, D)]

    def c_split(i):
        for g in range(8):
            r.c_send[i, g // 2, g % 2] = r.prod[2 * g + oc].astype(BF)
            r.c_own[i, g // 2, g % 2] = r.prod[2 * g + core].astype(BF)
        c0(i).start()

    def c_after0(i):
        c0(i).wait()
        for g in range(8):
            r.c_own[i, g // 2, g % 2] = (f(r.c_own[i, g // 2, g % 2]) + f(r.c_r0[i, g // 2, g % 2])).astype(BF)
        if i in Z_FIRST:
            c_line1(i)
        else:
            c1(i).start()

    def c_after1(i):
        c1(i).wait()
        for g in range(4):
            r.c_u[i, g] = (f(r.c_own[i, g, y]) + f(r.c_r1[i, g])).astype(BF)
        c_line1(i)

    def c_line1(i):
        @pl.when(end_z)
        def _():
            for n in range(3):
                c2(i, jnp.where(z == 0, 0, 1), jnp.where(z == 0, 3 - n, n)).start()

    def c_pass(i, way, t):
        c2(i, way, t).wait_recv()
        if i in Z_FIRST:
            r.c_own[i, t] = (f(r.c_own[i, t]) + f(r.z_r2[i, way, t])).astype(BF)
        else:
            r.c_u[i, t] = (f(r.c_u[i, t]) + f(r.c_r2[i, way, t])).astype(BF)
        c2(i, way, t).start()

    def c_line2(i):
        @pl.when(mid_z)
        def _():
            for n in range(2):
                c_pass(i, jnp.where(z == 1, 0, 1), jnp.where(z == 1, 3 - n, n))

    def c_line3(i):
        @pl.when(mid_z)
        def _():
            c_pass(i, jnp.where(z == 2, 0, 1), jnp.where(z == 2, 3, 0))

    def c_last(i):
        got = r.z_r2 if i in Z_FIRST else r.c_r2
        parts = ((oy, r.prod.at[0]), (y, c_target(i))) if i in Z_FIRST else ((None, c_target(i)),)
        for q, out in parts:
            out[...] = f(r.c_u[i, z]) if q is None else f(r.c_own[i, z, q])

        @pl.when(z > 0)
        def _():
            c2(i, 0, z).wait_recv()
            for q, out in parts:
                out[...] += f(got[i, 0, z]) if q is None else f(got[i, 0, z, q])

        @pl.when(z < 3)
        def _():
            c2(i, 1, z).wait_recv()
            for q, out in parts:
                out[...] += f(got[i, 1, z]) if q is None else f(got[i, 1, z, q])

        if i in Z_FIRST:
            r.z_v[i] = r.prod[0].astype(BF)
            z4(i).start()

        @pl.when(end_z)
        def _():
            for n in range(3):
                c2(i, jnp.where(z == 0, 0, 1), jnp.where(z == 0, 3 - n, n)).wait_send()

        @pl.when(mid_z)
        def _():
            for n in range(2):
                c2(i, jnp.where(z == 1, 0, 1), jnp.where(z == 1, 3 - n, n)).wait_send()
            c2(i, jnp.where(z == 2, 0, 1), jnp.where(z == 2, 3, 0)).wait_send()

    def z_last(i):
        z4(i).wait()
        c_target(i)[...] += f(r.z_r4[i])

    def d0(k):
        return send(r.d_send.at[k], r.d_r0.at[k], r.ds0.at[k], r.dr0.at[k], to_core)

    def d1(t):
        return send(r.d_own.at[t, oy], r.d_r1.at[t], r.ds1.at[t], r.dr1.at[t], to_y)

    def d2(way, t):
        return send(r.d_u.at[t], r.d_r2.at[way, t], r.ds2.at[way, t], r.dr2.at[way, t], at(core, y, z + 1 - 2 * way))

    def d_split(k):
        for q in range(2):
            for p in range(4):
                rows = slice(48 * p, 48 * p + 48)
                r.d_send[k, q, rows] = r.prod[(2 * q + oc) * 4 + p].astype(BF)
                r.d_own[k, q, rows] = r.prod[(2 * q + core) * 4 + p].astype(BF)
        d0(k).start()

    def d_after0(k):
        d0(k).wait()
        for q in range(2):
            r.d_own[k, q] = (f(r.d_own[k, q]) + f(r.d_r0[k, q])).astype(BF)
        d1(k).start()

    def d_after1(t):
        d1(t).wait()
        r.d_u[t] = (f(r.d_own[t, y]) + f(r.d_r1[t])).astype(BF)

        @pl.when((z == 0) & (t > 0))
        def _():
            d2(0, t).start()

        @pl.when((z == 3) & (t < 3))
        def _():
            d2(1, t).start()

    def d_pass(way, t):
        d2(way, t).wait_recv()
        r.d_u[t] = (f(r.d_u[t]) + f(r.d_r2[way, t])).astype(BF)
        d2(way, t).start()

    def d_line2(t):
        @pl.when((z == 1) & (t > 1))
        def _():
            d_pass(0, t)

        @pl.when((z == 2) & (t < 2))
        def _():
            d_pass(1, t)

    def d_line3(t):
        @pl.when((z == 2) & (t > 2))
        def _():
            d_pass(0, t)

        @pl.when((z == 1) & (t < 1))
        def _():
            d_pass(1, t)

    def d_last():
        r.g_down[...] = f(r.d_u[z])

        @pl.when(z > 0)
        def _():
            d2(0, z).wait_recv()
            r.g_down[...] += f(r.d_r2[0, z])

        @pl.when(z < 3)
        def _():
            d2(1, z).wait_recv()
            r.g_down[...] += f(r.d_r2[1, z])

        for t in range(4):
            @pl.when(z < t)
            def _():
                d2(0, t).wait_send()

            @pl.when(z > t)
            def _():
                d2(1, t).wait_send()

    peers = (to_core, to_y, to_z1, to_z2)

    def small_send(k):
        return send(r.small.at[k], r.small_r.at[k], r.ss.at[k], r.sr.at[k], peers[k])

    def small_step(k):
        small_send(k).wait()
        r.small[k + 1] = r.small[k] + r.small_r[k]
        if k < 3:
            small_send(k + 1).start()

    def small_out():
        total = r.small[4]
        per = D // 16
        pick = lambda n, at_: jnp.where(lax.broadcasted_iota(jnp.int32, (D, n), 0) == at_ + lax.broadcasted_iota(jnp.int32, (D, n), 1), 1.0, 0.0)
        vec = lax.dot_general(total, pick(per, dp * per), (((1,), (0,)), ((), ())), precision=lax.Precision.HIGHEST, preferred_element_type=F32)
        up = lax.dot_general(total, pick(4 * per, lax.rem(dp, 4) * (4 * per)), (((1,), (0,)), ((), ())), precision=lax.Precision.HIGHEST, preferred_element_type=F32)
        for n, out in enumerate((r.g_ga, r.g_sa, r.g_bd, r.g_gf, r.g_sf)):
            out[...] = vec[n:n + 1]
        bu = jnp.zeros((1, 4 * per), F32)
        for n in range(4):
            bu = bu + jnp.where(lax.div(dp, 4) == n, 1.0, 0.0) * up[5 + n:6 + n]
        r.g_bu[...] = bu

    plan = {}

    def later(slot, fn, *args):
        plan.setdefault(slot, []).append((fn, args))

    for n, (kind, i) in enumerate(ITEMS):
        if kind == BLOCK and i in Z_FIRST:
            stages = tuple(zip((c_after0, c_line2, c_line3, c_last, z_last), Z_WAITS))
        elif kind == BLOCK:
            stages = tuple(zip((c_after0, c_after1, c_line2, c_line3, c_last), WAITS))
        else:
            stages = tuple(zip((d_after0, d_after1, d_line2, d_line3), WAITS))
        for fn, wait in stages:
            later(n + wait, fn, i)
    later(max(n for n, item in enumerate(ITEMS) if item[0] == ROW_SET) + WAITS[4], d_last)
    for k in range(4):
        later(k + 1, small_step, k)

    for c in loads(0):
        c.start()
    r.small[0] = jnp.zeros((16, D), F32)
    r.small[0, 0:5] = jnp.sum(r.sm[...], axis=1)
    for n in range(4):
        r.small[0, 5 + n:6 + n] = jnp.sum(r.sbu[:, n * D:(n + 1) * D], axis=0, keepdims=True)
    pl.semaphore_wait(barrier, 5)
    small_send(0).start()
    for n in range(max(plan) + 1):
        if n < len(ITEMS):
            item = ITEMS[n]
            if n + 1 < len(ITEMS):
                for c in loads(n + 1):
                    c.start()
            for c in loads(n):
                c.wait()
            k = n % 2
            value = dot_tn(r.a_buf[k].reshape(4 * SEQ, D), r.b_buf[k].reshape(4 * SEQ, D))
            r.prod[...] = value.reshape(16, 48, D)
            (c_split if item[0] == BLOCK else d_split)(item[1])
        for fn, args in plan.get(n, ()):
            fn(*args)
    small_out()


def run_weights(operands):
    any_space, vmem = pl.BlockSpec(memory_space=pl.ANY), pl.BlockSpec(memory_space=pltpu.VMEM)
    shapes = [(48, 3 * D), (48, D), (48, FF), (192, D), (1, 48), (1, 48), (1, 192), (1, 48), (1, 48), (1, 48)]
    outs = pl.pallas_call(
        weights_kernel, out_shape=[jax.ShapeDtypeStruct(s, F32) for s in shapes],
        in_specs=[any_space] * 8 + [vmem] * 2, out_specs=[vmem] * len(shapes),
        scratch_shapes=[pltpu.VMEM(*v) for v in W_SCRATCH.values()] + [pltpu.SemaphoreType.DMA(v) for v in W_SEMS.values()],
        name="weights",
        compiler_params=pltpu.CompilerParams(collective_id=2, has_side_effects=True, vmem_limit_bytes=62 * 2**20),
    )(*operands)
    return types.SimpleNamespace(**dict(zip(W_OUT, outs)))


def weight_product(left, right):
    rows = left.shape[0] * left.shape[1]
    return lax.dot_general(
        left.reshape(rows, -1), right.reshape(rows, -1), (((0,), (0,)), ((), ())), preferred_element_type=F32
    )


def body(
    sizes, tokens, cotangent, segment_ids, feature_ids, w_qkv, w_out, gain_attn, shift_attn, w_up, bias_up, w_down, bias_down, gain_ffn, shift_ffn
):
    sec = lax.axis_index("section")
    micro = segment_ids.shape[0]
    comb = segment_ids * 128 + feature_ids * (1 - sec)
    weights = (w_qkv[0], w_out[0], gain_attn, shift_attn, w_up[0], bias_up, w_down[0], bias_down, gain_ffn, shift_ffn)
    (h, din, sm, sbu), o = run_pipeline(tokens, cotangent, comb, weights, micro)
    h, din = h.reshape(1, micro * SEQ, D), din.reshape(1, micro * SEQ, D)
    if sizes == (2, 16) and micro == 4:
        g = run_weights((o.x_all, o.dq, o.ctx, o.out_in, o.nl, o.up_in, o.act, o.down_in, sm, sbu))
        return (
            h, din, g.g_qkv[None], g.g_out[None], g.g_ga, g.g_sa, g.g_up[None], g.g_bu, g.g_down[None], g.g_bd, g.g_gf, g.g_sf,
        )
    sm = jnp.sum(sm, axis=1)
    sbu = jnp.sum(sbu, axis=0)
    scatter = lambda v: lax.psum_scatter(v, "dp", scatter_dimension=0, tiled=True)[None]
    g_qkv, g_out = scatter(weight_product(o.x_all, o.dq)), scatter(weight_product(o.ctx, o.out_in))
    g_up, g_down = scatter(weight_product(o.nl, o.up_in)), scatter(weight_product(o.act, o.down_in))
    return (h, din, g_qkv, g_out, scatter(sm[0]), scatter(sm[1]), g_up, scatter(sbu), g_down, scatter(sm[2]), scatter(sm[3]), scatter(sm[4]))


def solution(mesh):
    rows, mat, vec = PartitionSpec("dp", None), PartitionSpec("section", None, None), PartitionSpec("section", None)
    in_specs = (rows,) * 4 + (mat, mat, vec, vec, mat, vec, mat, vec, vec, vec)
    big, small = PartitionSpec("section", "dp", None), PartitionSpec("section", "dp")
    out_specs = (big, big, big, big, small, small, big, small, big, small, small, small)
    return jax.shard_map(
        functools.partial(body, (mesh.shape["section"], mesh.shape["dp"])), mesh=mesh, in_specs=in_specs, out_specs=out_specs, check_vma=False
    )
```

```python
import functools
import types

import jax
import jax.numpy as jnp
from jax import lax
from jax.experimental import pallas as pl
from jax.experimental.pallas import tpu as pltpu
from jax.sharding import PartitionSpec

BF, F32 = jnp.bfloat16, jnp.float32
SEQ, D, FF, HEAD = 512, 768, 3072, 64
QB, NQ, KW = 128, 4, 384
QUADS, QW = 3, 256
FC, RB = 512, 256
EPS = 1e-5
C0, C1 = 0.7978845608028654, 0.044715
MESH = pl.DeviceIdType.MESH


def dot(a, b):
    return lax.dot_general(a, b, (((1,), (0,)), ((), ())), preferred_element_type=F32)


def dot_nt(a, b):
    return lax.dot_general(a, b, (((1,), (1,)), ((), ())), preferred_element_type=F32)


def dot_tn(a, b):
    return lax.dot_general(a, b, (((0,), (0,)), ((), ())), preferred_element_type=F32)


def keys_of(block, reach):
    return max(0, block * QB - reach), min(SEQ, (block + 1) * QB + reach)


REACH = (16, 128)


def row_blocks(size=RB):
    return [slice(n * size, (n + 1) * size) for n in range(SEQ // size)]


def norm_rows(v):
    c = v - jnp.mean(v, axis=-1, keepdims=True)
    r = lax.rsqrt(jnp.mean(c * c, axis=-1, keepdims=True) + EPS)
    return c * r, r


def norm_back(e, n, r):
    return r * (e - jnp.mean(e, axis=-1, keepdims=True) - n * jnp.mean(e * n, axis=-1, keepdims=True))


def column_sums(v):
    return jnp.sum(v.reshape(v.shape[0] // 8, 8, v.shape[1]), axis=0)


def make_bias(seg, feat, bias, reach, use_feat):
    row = (seg * 128 + feat * use_feat).astype(F32)
    col = jnp.transpose(jnp.broadcast_to(row, (QB, SEQ)))
    for qb in range(NQ):
        lo, hi = keys_of(qb, reach)
        same = col[lo:hi, :] == row[:, qb * QB:(qb + 1) * QB]
        bias[qb, 0:hi - lo, :] = jnp.where(same, 0.0, -1e30).astype(F32)


def head_lanes():
    lane = lax.broadcasted_iota(jnp.int32, (1, QW), 1)
    return [jnp.where((lane >= HEAD * i) & (lane < HEAD * (i + 1)), 1.0, 0.0).astype(BF) for i in range(4)]


def by_head(v, masks):
    return jnp.concatenate([v * m for m in masks], axis=0)


def f_qkv(x, w_qkv, qkv):
    qkv[:, 0:D] = (dot(x[...], w_qkv[:, 0:D]) * 0.125).astype(BF)
    for j in range(1, 3):
        qkv[:, j * D:(j + 1) * D] = dot(x[...], w_qkv[:, j * D:(j + 1) * D]).astype(BF)


def f_attention(qkv, bias, probs, ctx, inv, reach):
    first = lax.broadcasted_iota(jnp.int32, (QB, 128), 1) < HEAD
    masks = head_lanes()
    ones = jnp.ones((KW, 128), BF)

    def quad(p, carry):
        base = pl.multiple_of(p * QW, QW)
        scores = {}

        def begin(qb):
            lo, hi = keys_of(qb, reach)
            q = qkv[qb * QB:(qb + 1) * QB, pl.ds(base, QW)]
            k = qkv[lo:hi, pl.ds(pl.multiple_of(D + base, QW), QW)]
            scores[qb] = dot_nt(k, by_head(q, masks))

        def finish(qb):
            lo, hi = keys_of(qb, reach)
            kw, qs = hi - lo, slice(qb * QB, (qb + 1) * QB)
            v = qkv[lo:hi, pl.ds(pl.multiple_of(2 * D + base, QW), QW)]
            all_four, b, e = scores.pop(qb), bias[qb, 0:kw, :], []
            for hd in range(4):
                s = all_four[:, hd * QB:(hd + 1) * QB] + b
                e.append(jnp.exp((s - jnp.max(s, axis=0, keepdims=True)).astype(BF)))
                probs[p, qb, 0:kw, hd * QB:(hd + 1) * QB] = e[hd]
            for n in range(2):
                right = jnp.concatenate([v[:, n * 128:(n + 1) * 128], ones[:kw]], axis=1)
                o = dot_tn(jnp.concatenate(e[2 * n:2 * n + 2], axis=1), right)
                value = jnp.where(first, o[:QB, :128], o[QB:, :128])
                recip = 1.0 / jnp.where(first, o[:QB, 128:], o[QB:, 128:])
                inv[qs, pl.ds(base + n * 128, 128)] = recip
                ctx[qs, pl.ds(base + n * 128, 128)] = (value * recip).astype(BF)

        begin(0)
        begin(1)
        for qb in range(NQ):
            if qb + 2 < NQ:
                begin(qb + 2)
            finish(qb)
        return carry

    lax.fori_loop(0, QUADS, quad, 0)


def f_mid(x, ctx, w_out, gain, shift, n1, nl, r1, nf):
    for rs in row_blocks():
        n, r = norm_rows(x[rs, :].astype(F32) + dot(ctx[rs, :], w_out[...]))
        out = n * gain[...] + shift[...]
        n1[rs, :] = n.astype(BF)
        r1[rs, :] = jnp.broadcast_to(r, (RB, 128))
        nl[rs, :] = out.astype(BF)
        nf[rs, :] = out


def gelu_both(p):
    p2 = p * p
    t = jnp.tanh(p * (C0 + (C0 * C1) * p2))
    h = 0.5 + 0.5 * t
    return p * h, h + (p * (C0 + (3 * C0 * C1) * p2)) * (0.5 - 0.5 * (t * t))


def f_ffn(nl, nf, w_up, b_up, w_down, b_down, gain, shift, dg, act, n2, r2, h):
    for c in range(FF // FC):
        cs = slice(c * FC, (c + 1) * FC)
        a, d = gelu_both(dot(nl[...], w_up[:, cs]) + b_up[:, cs])
        act[:, cs] = a.astype(BF)
        dg[:, cs] = d.astype(BF)
    for rs in row_blocks():
        n, r = norm_rows(nf[rs, :] + dot(act[rs, :], w_down[...]) + b_down[...])
        n2[rs, :] = n.astype(BF)
        r2[rs, :] = jnp.broadcast_to(r, (RB, 128))
        h[rs, :] = (n * gain[...] + shift[...]).astype(BF)


def b_ffn(g, n2, r2, gain_ffn, w_down, dg, w_up, n1, r1, gain_attn, down_in, up_in, d_ffn, d_attn, out_in, sm, sbu):
    for rs in row_blocks():
        grad, n, r = g[rs, :].astype(F32), n2[rs, :].astype(F32), r2[rs, 0:1]
        d = norm_back(grad * gain_ffn[...], n, r)
        low = d.astype(BF)
        down_in[rs, :] = low
        d_ffn[rs, :] = d
        sm[3] += column_sums(grad * n)
        sm[4] += column_sums(grad)
        sm[2] += column_sums(low.astype(F32))
    for c in range(FF // FC):
        cs = slice(c * FC, (c + 1) * FC)
        u = (dot_nt(down_in[...], w_down[cs, :]) * dg[:, cs].astype(F32)).astype(BF)
        up_in[:, cs] = u
        sbu[:, cs] += column_sums(u.astype(F32))
    for rs in row_blocks():
        grad = d_ffn[rs, :] + dot_nt(up_in[rs, :], w_up[...])
        n, r = n1[rs, :].astype(F32), r1[rs, 0:1]
        d = norm_back(grad * gain_attn[...], n, r)
        d_attn[rs, :] = d
        out_in[rs, :] = d.astype(BF)
        sm[0] += column_sums(grad * n)
        sm[1] += column_sums(grad)


def b_attention(qkv, probs, ctx, d_ctx, d_qkv, reach):
    first = lax.broadcasted_iota(jnp.int32, (QB, 128), 1) < HEAD
    masks = head_lanes()
    pick = jnp.where(lax.broadcasted_iota(jnp.int32, (8, QW), 1) // HEAD == lax.broadcasted_iota(jnp.int32, (8, QW), 0), 1.0, 0.0).astype(BF)
    edges = sorted({e for qb in range(NQ) for e in keys_of(qb, reach)})

    def quad(p, carry):
        base = pl.multiple_of(p * QW, QW)
        kb, vb = pl.multiple_of(D + base, QW), pl.multiple_of(2 * D + base, QW)
        both = (d_ctx[:, pl.ds(base, QW)].astype(F32) * ctx[:, pl.ds(base, QW)].astype(F32)).astype(BF)
        delta = dot_nt(pick, both)
        d_prob, d_k, d_v = {}, {}, {}

        def begin(qb):
            lo, hi = keys_of(qb, reach)
            do = d_ctx[qb * QB:(qb + 1) * QB, pl.ds(base, QW)]
            d_prob[qb] = dot_nt(qkv[lo:hi, pl.ds(vb, QW)], by_head(do, masks))

        def finish(qb):
            lo, hi = keys_of(qb, reach)
            kw, qs = hi - lo, slice(qb * QB, (qb + 1) * QB)
            all_four, e, ds = d_prob.pop(qb), probs[p, qb, 0:kw, :], []
            for hd in range(4):
                hs = slice(hd * QB, (hd + 1) * QB)
                ds.append((e[:, hs].astype(F32) * (all_four[:, hs] - delta[hd:hd + 1, qs])).astype(BF))
            ds = jnp.concatenate(ds, axis=1)
            d_v[qb] = dot(e, by_head(d_ctx[qs, pl.ds(base, QW)], masks))
            d_k[qb] = dot(ds, by_head(qkv[qs, pl.ds(base, QW)], masks))
            k = qkv[lo:hi, pl.ds(kb, QW)]
            for n in range(2):
                o = dot_tn(ds[:, n * 2 * QB:(n + 1) * 2 * QB], k[:, n * 128:(n + 1) * 128])
                d_qkv[qs, pl.ds(base + n * 128, 128)] = (jnp.where(first, o[:QB], o[QB:]) * 0.125).astype(BF)

        def flush(done):
            low = keys_of(done, reach)[0]
            high = keys_of(done + 1, reach)[0] if done + 1 < NQ else SEQ
            for a, b in zip(edges, edges[1:]):
                if low <= a and b <= high:
                    for parts, col in ((d_k, kb), (d_v, vb)):
                        pieces = [parts[n][a - keys_of(n, reach)[0]:b - keys_of(n, reach)[0]] for n in parts if keys_of(n, reach)[0] <= a and b <= keys_of(n, reach)[1]]
                        d_qkv[a:b, pl.ds(col, QW)] = functools.reduce(lambda v, w: v + w, pieces).astype(BF)

        begin(0)
        begin(1)
        for qb in range(NQ):
            if qb + 2 < NQ:
                begin(qb + 2)
            finish(qb)
            flush(qb)
        return carry

    lax.fori_loop(0, QUADS, quad, 0)


def b_input(d_qkv, w_qkv, d_attn, d_in):
    for rs in row_blocks():
        d_in[rs, :] = (d_attn[rs, :] + dot_nt(d_qkv[rs, :], w_qkv[...])).astype(BF)


def arrays(**named):
    return named


SAVED = arrays(
    qkv=((SEQ, 3 * D), BF), probs=((QUADS, NQ, KW, 4 * QB), BF), ctx=((SEQ, D), BF), inv=((SEQ, D), F32), n1=((SEQ, D), BF), r1=((SEQ, 128), F32),
    nl=((SEQ, D), BF), dg=((SEQ, FF), BF), act=((SEQ, FF), BF), n2=((SEQ, D), BF), r2=((SEQ, 128), F32),
)
ROWS = arrays(down_in=((SEQ, D), BF), up_in=((SEQ, FF), BF), out_in=((SEQ, D), BF), dq=((SEQ, 3 * D), BF))
EARLY_BOTH, EARLY_ONE = tuple(arrays(ctx=0, nl=0)), tuple(arrays(qkv=0, probs=0, inv=0, n1=0, r1=0))
LATE_ONE = tuple(arrays(dg=0, n2=0, r2=0))
RELOADED = tuple(k for k in SAVED if k not in tuple(arrays(nl=0, act=0)))
WEIGHTS = arrays(wqkv=((D, 3 * D), BF), wout=((D, D), BF), wup=((D, FF), BF), wdown=((FF, D), BF))
INPUTS = arrays(tokens=0, cot=0, seg=0, feat=0, ga=0, sa=0, bu=0, bd=0, gf=0, sf=0)
SCRATCH = arrays(
    io=((8, SEQ, D), BF), nf=((SEQ, D), F32), datt=((SEQ, D), F32), dctx=((SEQ, D), BF), ho=((SEQ, D), BF), din=((SEQ, D), BF),
    bias=((4, NQ, KW, QB), F32), **WEIGHTS, **SAVED, **ROWS,
)
SEMS = arrays(s_w=(4,), s_own=(2,), s_f=(len(SAVED),), s_l=(len(SAVED),), s_b=(len(ROWS),), s_x=(1,), s_ho=(1,), s_din=(1,), s_sh=(1,), s_sd=(1,), s_r=(4,))


def pipeline_kernel(micro, *refs):
    n_in, n_w, n_out = len(INPUTS), len(WEIGHTS), 5 + len(SAVED) + len(ROWS)
    r = types.SimpleNamespace(**dict(zip(INPUTS, refs)))
    w_hbm = dict(zip(WEIGHTS, refs[n_in:]))
    h_all, din_all, sm, sbu, x_all = refs[n_in + n_w:][:5]
    kept = dict(zip((*SAVED, *ROWS), refs[n_in + n_w + 5:]))
    scratch = dict(zip((*SCRATCH, *SEMS), refs[n_in + n_w + n_out:]))
    s = types.SimpleNamespace(**scratch)
    sec, dp = lax.axis_index("section"), lax.axis_index("dp")
    core = lax.rem(dp, 2)
    first_sec = sec == 0
    second_sec = jnp.logical_not(first_sec)
    partner = (1 - sec, dp)
    barrier = pltpu.get_barrier_semaphore()
    pl.semaphore_signal(barrier, inc=1, device_id=partner, device_id_type=MESH)

    def own_copy(src, part):
        rows = (pl.ds(0, 1), pl.ds(1, micro - 1))[part]
        return pltpu.make_async_copy(src.at[rows], s.io.at[rows], s.s_own.at[part])

    w_copies = [pltpu.make_async_copy(w_hbm[k], scratch[k], s.s_w.at[n]) for n, k in enumerate(WEIGHTS)]

    @pl.when(first_sec)
    def _():
        own_copy(r.tokens, 0).start()

    @pl.when(second_sec)
    def _():
        own_copy(r.cot, 0).start()

    for c in w_copies:
        c.start()

    @pl.when(first_sec)
    def _():
        own_copy(r.tokens, 1).start()

    @pl.when(second_sec)
    def _():
        own_copy(r.cot, 1).start()

    sm[...] = jnp.zeros_like(sm)
    sbu[...] = jnp.zeros_like(sbu)

    def bias_of(mb, reach):
        make_bias(r.seg[pl.ds(mb, 1), :], r.feat[pl.ds(mb, 1), :], s.bias.at[mb], reach, 1 if reach == REACH[0] else 0)

    @pl.when(first_sec)
    def _():
        bias_of(0, REACH[0])

    @pl.when(second_sec)
    def _():
        lax.fori_loop(0, micro, lambda mb, c: (bias_of(mb, REACH[1]), c)[1], 0)

    own_copy(r.tokens, 0).wait()
    w_copies[0].wait()
    pl.semaphore_wait(barrier, 1)

    order = tuple(SAVED)

    def save(k, mb):
        return pltpu.make_async_copy(scratch[k], kept[k].at[mb], s.s_f.at[order.index(k)])

    def load(k, mb):
        return pltpu.make_async_copy(kept[k].at[mb], scratch[k], s.s_l.at[order.index(k)])

    def save_rows(k, mb):
        return pltpu.make_async_copy(scratch[k], kept[k].at[mb], s.s_b.at[tuple(ROWS).index(k)])

    def save_x(mb):
        return pltpu.make_async_copy(s.io.at[mb + micro * sec], x_all.at[mb], s.s_x.at[0])

    def save_act(mb):
        return save(order[8], mb)

    def save_h(mb):
        return pltpu.make_async_copy(s.ho, h_all.at[mb], s.s_ho.at[0])

    def save_din(mb):
        return pltpu.make_async_copy(s.din, din_all.at[mb], s.s_din.at[0])

    def send(src, mb, sem):
        return pltpu.make_async_remote_copy(
            src_ref=src, dst_ref=s.io.at[micro + mb], send_sem=sem.at[0], recv_sem=s.s_r.at[mb], device_id=partner, device_id_type=MESH
        )

    def send_h(mb):
        return send(s.ho, mb, s.s_sh)

    def send_din(mb):
        return send(s.din, mb, s.s_sd)

    def step(t, carry):
        is_f = jnp.where(first_sec, t < micro, lax.rem(t, 2) == 0)
        mb = jnp.where(first_sec, lax.rem(t, micro), lax.div(t, 2))
        after_f = jnp.where(first_sec, (t >= 1) & (t <= micro), lax.rem(t, 2) == 1)
        prev = jnp.where(first_sec, lax.rem(t + micro - 1, micro), lax.div(t, 2))
        late_send = first_sec & (core == 1)

        def wait_late():
            save_act(prev).wait()
            save_h(prev).wait()

            @pl.when(first_sec)
            def _():
                for k in LATE_ONE:
                    save(k, prev).wait()
                send_h(prev).wait_send()

        @pl.when(t == 1)
        def _():
            own_copy(r.tokens, 1).wait()

        @pl.when(after_f)
        def _():
            for k in EARLY_BOTH:
                save(k, prev).wait()
            save_x(prev).wait()

            @pl.when(first_sec)
            def _():
                for k in EARLY_ONE:
                    save(k, prev).wait()

        @pl.when(is_f)
        def _():
            @pl.when(second_sec)
            def _():
                send_h(mb).wait_recv()

            save_x(mb).start()
            x = s.io.at[mb + micro * sec]
            f_qkv(x, s.wqkv, s.qkv)

            @pl.when(first_sec)
            def _():
                save(order[0], mb).start()
                f_attention(s.qkv, s.bias.at[mb], s.probs, s.ctx, s.inv, REACH[0])
                for k in EARLY_ONE[1:3]:
                    save(k, mb).start()

            @pl.when(second_sec)
            def _():
                f_attention(s.qkv, s.bias.at[mb], s.probs, s.ctx, s.inv, REACH[1])

            @pl.when(late_send & (t == 1))
            def _():
                send_h(0).start()

            save(EARLY_BOTH[0], mb).start()

            @pl.when(t == 0)
            def _():
                for c in w_copies[1:]:
                    c.wait()

            f_mid(x, s.ctx, s.wout, r.ga, r.sa, s.n1, s.nl, s.r1, s.nf)
            save(EARLY_BOTH[1], mb).start()

            @pl.when(first_sec)
            def _():
                for k in EARLY_ONE[3:]:
                    save(k, mb).start()

            @pl.when(after_f)
            def _():
                wait_late()

            f_ffn(s.nl, s.nf, s.wup, r.bu, s.wdown, r.bd, r.gf, r.sf, s.dg, s.act, s.n2, s.r2, s.ho)

            @pl.when(first_sec & jnp.logical_not(late_send & (t == 0)))
            def _():
                send_h(mb).start()

            save_act(mb).start()
            save_h(mb).start()

            @pl.when(first_sec)
            def _():
                for k in LATE_ONE:
                    save(k, mb).start()

                @pl.when(t < micro - 1)
                def _():
                    bias_of(mb + 1, REACH[0])

        @pl.when(jnp.logical_not(is_f))
        def _():
            @pl.when(first_sec)
            def _():
                @pl.when(after_f)
                def _():
                    wait_late()
                    for k in RELOADED:
                        load(k, mb).start()

                for k in RELOADED:
                    load(k, mb).wait()
                send_din(mb).wait_recv()

            not_first_b = jnp.where(first_sec, t > micro, t > 1)
            before = mb - 1

            @pl.when(not_first_b)
            def _():
                for k in ROWS:
                    save_rows(k, before).wait()
                save_din(before).wait()

                @pl.when(second_sec)
                def _():
                    send_din(before).wait_send()

            g = s.io.at[mb + micro * (1 - sec)]
            b_ffn(g, s.n2, s.r2, r.gf, s.wdown, s.dg, s.wup, s.n1, s.r1, r.ga, s.down_in, s.up_in, s.nf, s.datt, s.out_in, sm, sbu)
            for k in tuple(ROWS)[:3]:
                save_rows(k, mb).start()

            @pl.when(second_sec)
            def _():
                wait_late()

            s.dctx[...] = (dot_nt(s.out_in[...], s.wout[...]) * s.inv[...]).astype(BF)

            @pl.when(first_sec)
            def _():
                b_attention(s.qkv, s.probs, s.ctx, s.dctx, s.dq, REACH[0])

            @pl.when(second_sec)
            def _():
                b_attention(s.qkv, s.probs, s.ctx, s.dctx, s.dq, REACH[1])

            save_rows(tuple(ROWS)[3], mb).start()
            b_input(s.dq, s.wqkv, s.datt, s.din)

            @pl.when(second_sec)
            def _():
                send_din(mb).start()

            save_din(mb).start()

            @pl.when(first_sec & (mb < micro - 1))
            def _():
                for k in RELOADED:
                    load(k, mb + 1).start()

        return carry

    lax.fori_loop(0, 2 * micro, step, 0)
    last = micro - 1
    for k in ROWS:
        save_rows(k, last).wait()
    save_din(last).wait()

    @pl.when(second_sec)
    def _():
        send_din(last).wait_send()


def run_pipeline(tokens, cot, seg, feat, weights, micro):
    w_qkv, w_out, gain_attn, shift_attn, w_up, bias_up, w_down, bias_down, gain_ffn, shift_ffn = weights
    any_space, vmem = pl.BlockSpec(memory_space=pl.ANY), pl.BlockSpec(memory_space=pltpu.VMEM)
    operands = (
        tokens.reshape(micro, SEQ, D), cot.reshape(micro, SEQ, D), seg, feat,
        gain_attn, shift_attn, bias_up, bias_down, gain_ffn, shift_ffn, w_qkv, w_out, w_up, w_down,
    )
    in_specs = [any_space] * 2 + [vmem] * 8 + [any_space] * 4
    out_shape = [
        jax.ShapeDtypeStruct((micro, SEQ, D), BF), jax.ShapeDtypeStruct((micro, SEQ, D), BF),
        jax.ShapeDtypeStruct((5, 8, D), F32), jax.ShapeDtypeStruct((8, FF), F32), jax.ShapeDtypeStruct((micro, SEQ, D), BF),
    ] + [jax.ShapeDtypeStruct((micro,) + shape, dtype) for shape, dtype in (*SAVED.values(), *ROWS.values())]
    out_specs = [any_space] * 2 + [vmem] * 2 + [any_space] * (len(out_shape) - 4)
    scratch = [pltpu.VMEM(*v) for v in SCRATCH.values()] + [pltpu.SemaphoreType.DMA(v) for v in SEMS.values()]
    outs = pl.pallas_call(
        functools.partial(pipeline_kernel, micro), out_shape=out_shape, in_specs=in_specs, out_specs=out_specs, scratch_shapes=scratch,
        name="pipeline",
        compiler_params=pltpu.CompilerParams(collective_id=1, has_side_effects=True, vmem_limit_bytes=63 * 2**20),
    )(*operands)
    return outs[:4], types.SimpleNamespace(x_all=outs[4], **dict(zip((*SAVED, *ROWS), outs[5:])))


WAITS, Z_WAITS, D_WAITS, LAST = (1, 6, 7, 8, 20), (1, 3, 6, 12, 20), (1, 4, 7, 11), 20
Z_FIRST = (0, 1)
BLOCK, ROW_SET = 0, 1
ITEMS = (
    (ROW_SET, 1), (BLOCK, 1), (BLOCK, 2), (BLOCK, 4), (BLOCK, 0), (ROW_SET, 3), (ROW_SET, 0), (ROW_SET, 2), (BLOCK, 5), (BLOCK, 7), (BLOCK, 6), (BLOCK, 3),
)
W_IN = arrays(x_all=0, dq=0, ctx=0, out_in=0, nl=0, up_in=0, act=0, down_in=0, sm=0, sbu=0)
W_OUT = arrays(g_qkv=0, g_out=0, g_up=0, g_down=0, g_ga=0, g_sa=0, g_bu=0, g_bd=0, g_gf=0, g_sf=0)
NC = 8
W_SCRATCH = arrays(
    a_buf=((2, 4, SEQ, D), BF), b_buf=((2, 4, SEQ, D), BF), prod=((16, 48, D), F32),
    c_send=((NC, 4, 2, 48, D), BF), c_own=((NC, 4, 2, 48, D), BF), c_r0=((NC, 4, 2, 48, D), BF),
    c_r1=((NC, 4, 48, D), BF), c_u=((NC, 4, 48, D), BF), c_r2=((NC, 2, 4, 48, D), BF),
    d_send=((4, 2, 192, D), BF), d_own=((4, 2, 192, D), BF), d_r0=((4, 2, 192, D), BF),
    d_r1=((4, 192, D), BF), d_u=((4, 192, D), BF), d_r2=((2, 4, 192, D), BF),
    z_r2=((2, 2, 4, 2, 48, D), BF), z_v=((2, 48, D), BF), z_r4=((2, 48, D), BF),
    small=((5, 16, D), F32), small_r=((4, 16, D), F32),
)
W_SEMS = arrays(
    l_a=(2,), l_b=(2,), cs0=(NC,), cr0=(NC,), cs1=(NC,), cr1=(NC,), cs2=(NC, 2, 4), cr2=(NC, 2, 4),
    ds0=(4,), dr0=(4,), ds1=(4,), dr1=(4,), ds2=(2, 4), dr2=(2, 4), ss=(4,), sr=(4,), zs4=(2,), zr4=(2,),
)


def weights_kernel(*refs):
    r = types.SimpleNamespace(**dict(zip((*W_IN, *W_OUT, *W_SCRATCH, *W_SEMS), refs)))
    sec, dp = lax.axis_index("section"), lax.axis_index("dp")
    core, y, z = lax.rem(dp, 2), lax.rem(lax.div(dp, 2), 2), lax.div(dp, 4)
    oc, oy = 1 - core, 1 - y
    at = lambda c_, y_, z_: (sec, z_ * 4 + y_ * 2 + c_)
    to_core, to_y = at(oc, y, z), at(core, oy, z)
    to_z1, to_z2 = at(core, y, z + 1 - 2 * lax.rem(z, 2)), at(core, y, lax.rem(z + 2, 4))
    end_z, mid_z = (z == 0) | (z == 3), (z == 1) | (z == 2)
    barrier = pltpu.get_barrier_semaphore()
    for peer in (to_core, to_y, at(core, y, lax.rem(z + 1, 4)), to_z2, at(core, y, lax.rem(z + 3, 4))):
        pl.semaphore_signal(barrier, inc=1, device_id=peer, device_id_type=MESH)

    def send(src, dst, s, q, peer):
        return pltpu.make_async_remote_copy(src_ref=src, dst_ref=dst, send_sem=s, recv_sem=q, device_id=peer, device_id_type=MESH)

    def block(ref, j):
        return ref if ref.shape[2] == D else ref.at[:, :, pl.ds(j, D)]

    def operands(item):
        i = item[1]
        if item[0] == ROW_SET:
            return block(r.act, i * D), block(r.down_in, 0)
        if i < 3:
            return block(r.x_all, 0), block(r.dq, i * D)
        if i == 3:
            return block(r.ctx, 0), block(r.out_in, 0)
        return block(r.nl, 0), block(r.up_in, (i - 4) * D)

    def loads(n):
        a, b = operands(ITEMS[n])
        k = n % 2
        return pltpu.make_async_copy(a, r.a_buf.at[k], r.l_a.at[k]), pltpu.make_async_copy(b, r.b_buf.at[k], r.l_b.at[k])

    f = lambda v: v.astype(F32)
    def c0(i):
        return send(r.c_send.at[i], r.c_r0.at[i], r.cs0.at[i], r.cr0.at[i], to_core)

    def c1(i):
        return send(r.c_own.at[i, :, oy], r.c_r1.at[i], r.cs1.at[i], r.cr1.at[i], to_y)

    def c2(i, way, t):
        src, dst = (r.c_own, r.z_r2) if i in Z_FIRST else (r.c_u, r.c_r2)
        return send(src.at[i, t], dst.at[i, way, t], r.cs2.at[i, way, t], r.cr2.at[i, way, t], at(core, y, z + 1 - 2 * way))

    def z4(i):
        return send(r.z_v.at[i], r.z_r4.at[i], r.zs4.at[i], r.zr4.at[i], to_y)

    def c_target(i):
        if i < 3:
            return r.g_qkv.at[:, pl.ds(i * D, D)]
        return r.g_out if i == 3 else r.g_up.at[:, pl.ds((i - 4) * D, D)]

    def c_split(i):
        for g in range(8):
            r.c_send[i, g // 2, g % 2] = r.prod[2 * g + oc].astype(BF)
            r.c_own[i, g // 2, g % 2] = r.prod[2 * g + core].astype(BF)
        c0(i).start()

    def c_after0(i):
        c0(i).wait()
        for g in range(8):
            r.c_own[i, g // 2, g % 2] = (f(r.c_own[i, g // 2, g % 2]) + f(r.c_r0[i, g // 2, g % 2])).astype(BF)
        if i in Z_FIRST:
            c_line1(i)
        else:
            c1(i).start()

    def c_after1(i):
        c1(i).wait()
        for g in range(4):
            r.c_u[i, g] = (f(r.c_own[i, g, y]) + f(r.c_r1[i, g])).astype(BF)
        c_line1(i)

    def c_line1(i):
        @pl.when(end_z)
        def _():
            for n in range(3):
                c2(i, jnp.where(z == 0, 0, 1), jnp.where(z == 0, 3 - n, n)).start()

    def c_pass(i, way, t):
        c2(i, way, t).wait_recv()
        if i in Z_FIRST:
            r.c_own[i, t] = (f(r.c_own[i, t]) + f(r.z_r2[i, way, t])).astype(BF)
        else:
            r.c_u[i, t] = (f(r.c_u[i, t]) + f(r.c_r2[i, way, t])).astype(BF)
        c2(i, way, t).start()

    def c_line2(i):
        @pl.when(mid_z)
        def _():
            for n in range(2):
                c_pass(i, jnp.where(z == 1, 0, 1), jnp.where(z == 1, 3 - n, n))

    def c_line3(i):
        @pl.when(mid_z)
        def _():
            c_pass(i, jnp.where(z == 2, 0, 1), jnp.where(z == 2, 3, 0))

    def c_last(i):
        got = r.z_r2 if i in Z_FIRST else r.c_r2
        parts = ((oy, r.prod.at[0]), (y, c_target(i))) if i in Z_FIRST else ((None, c_target(i)),)
        for q, out in parts:
            out[...] = f(r.c_u[i, z]) if q is None else f(r.c_own[i, z, q])

        @pl.when(z > 0)
        def _():
            c2(i, 0, z).wait_recv()
            for q, out in parts:
                out[...] += f(got[i, 0, z]) if q is None else f(got[i, 0, z, q])

        @pl.when(z < 3)
        def _():
            c2(i, 1, z).wait_recv()
            for q, out in parts:
                out[...] += f(got[i, 1, z]) if q is None else f(got[i, 1, z, q])

        if i in Z_FIRST:
            r.z_v[i] = r.prod[0].astype(BF)
            z4(i).start()

        @pl.when(end_z)
        def _():
            for n in range(3):
                c2(i, jnp.where(z == 0, 0, 1), jnp.where(z == 0, 3 - n, n)).wait_send()

        @pl.when(mid_z)
        def _():
            for n in range(2):
                c2(i, jnp.where(z == 1, 0, 1), jnp.where(z == 1, 3 - n, n)).wait_send()
            c2(i, jnp.where(z == 2, 0, 1), jnp.where(z == 2, 3, 0)).wait_send()

    def z_last(i):
        z4(i).wait()
        c_target(i)[...] += f(r.z_r4[i])

    def d0(k):
        return send(r.d_send.at[k], r.d_r0.at[k], r.ds0.at[k], r.dr0.at[k], to_core)

    def d1(t):
        return send(r.d_own.at[t, oy], r.d_r1.at[t], r.ds1.at[t], r.dr1.at[t], to_y)

    def d2(way, t):
        return send(r.d_u.at[t], r.d_r2.at[way, t], r.ds2.at[way, t], r.dr2.at[way, t], at(core, y, z + 1 - 2 * way))

    def d_split(k):
        for q in range(2):
            for p in range(4):
                rows = slice(48 * p, 48 * p + 48)
                r.d_send[k, q, rows] = r.prod[(2 * q + oc) * 4 + p].astype(BF)
                r.d_own[k, q, rows] = r.prod[(2 * q + core) * 4 + p].astype(BF)
        d0(k).start()

    def d_after0(k):
        d0(k).wait()
        for q in range(2):
            r.d_own[k, q] = (f(r.d_own[k, q]) + f(r.d_r0[k, q])).astype(BF)
        d1(k).start()

    def d_after1(t):
        d1(t).wait()
        r.d_u[t] = (f(r.d_own[t, y]) + f(r.d_r1[t])).astype(BF)

        @pl.when((z == 0) & (t > 0))
        def _():
            d2(0, t).start()

        @pl.when((z == 3) & (t < 3))
        def _():
            d2(1, t).start()

    def d_pass(way, t):
        d2(way, t).wait_recv()
        r.d_u[t] = (f(r.d_u[t]) + f(r.d_r2[way, t])).astype(BF)
        d2(way, t).start()

    def d_line2(t):
        @pl.when((z == 1) & (t > 1))
        def _():
            d_pass(0, t)

        @pl.when((z == 2) & (t < 2))
        def _():
            d_pass(1, t)

    def d_line3(t):
        @pl.when((z == 2) & (t > 2))
        def _():
            d_pass(0, t)

        @pl.when((z == 1) & (t < 1))
        def _():
            d_pass(1, t)

    def d_last():
        r.g_down[...] = f(r.d_u[z])

        @pl.when(z > 0)
        def _():
            d2(0, z).wait_recv()
            r.g_down[...] += f(r.d_r2[0, z])

        @pl.when(z < 3)
        def _():
            d2(1, z).wait_recv()
            r.g_down[...] += f(r.d_r2[1, z])

        for t in range(4):
            @pl.when(z < t)
            def _():
                d2(0, t).wait_send()

            @pl.when(z > t)
            def _():
                d2(1, t).wait_send()

    peers = (to_core, to_y, to_z1, to_z2)

    def small_send(k):
        return send(r.small.at[k], r.small_r.at[k], r.ss.at[k], r.sr.at[k], peers[k])

    def small_step(k):
        small_send(k).wait()
        r.small[k + 1] = r.small[k] + r.small_r[k]
        if k < 3:
            small_send(k + 1).start()

    def small_out():
        total = r.small[4]
        per = D // 16
        pick = lambda n, at_: jnp.where(lax.broadcasted_iota(jnp.int32, (D, n), 0) == at_ + lax.broadcasted_iota(jnp.int32, (D, n), 1), 1.0, 0.0)
        vec = lax.dot_general(total, pick(per, dp * per), (((1,), (0,)), ((), ())), precision=lax.Precision.HIGHEST, preferred_element_type=F32)
        up = lax.dot_general(total, pick(4 * per, lax.rem(dp, 4) * (4 * per)), (((1,), (0,)), ((), ())), precision=lax.Precision.HIGHEST, preferred_element_type=F32)
        for n, out in enumerate((r.g_ga, r.g_sa, r.g_bd, r.g_gf, r.g_sf)):
            out[...] = vec[n:n + 1]
        bu = jnp.zeros((1, 4 * per), F32)
        for n in range(4):
            bu = bu + jnp.where(lax.div(dp, 4) == n, 1.0, 0.0) * up[5 + n:6 + n]
        r.g_bu[...] = bu

    plan = {}

    def later(slot, fn, *args):
        plan.setdefault(slot, []).append((fn, args))

    for n, (kind, i) in enumerate(ITEMS):
        if kind == BLOCK and i in Z_FIRST:
            stages = tuple(zip((c_after0, c_line2, c_line3, c_last, z_last), Z_WAITS))
        elif kind == BLOCK:
            stages = tuple(zip((c_after0, c_after1, c_line2, c_line3, c_last), WAITS))
        else:
            stages = tuple(zip((d_after0, d_after1, d_line2, d_line3), D_WAITS))
        for fn, wait in stages:
            later(n + wait, fn, i)
    later(max(n for n, item in enumerate(ITEMS) if item[0] == ROW_SET) + LAST, d_last)
    for k in range(4):
        later(k + 1, small_step, k)

    for c in loads(0):
        c.start()
    r.small[0] = jnp.zeros((16, D), F32)
    r.small[0, 0:5] = jnp.sum(r.sm[...], axis=1)
    for n in range(4):
        r.small[0, 5 + n:6 + n] = jnp.sum(r.sbu[:, n * D:(n + 1) * D], axis=0, keepdims=True)
    pl.semaphore_wait(barrier, 5)
    small_send(0).start()
    for n in range(max(plan) + 1):
        if n < len(ITEMS):
            item = ITEMS[n]
            if n + 1 < len(ITEMS):
                for c in loads(n + 1):
                    c.start()
            for c in loads(n):
                c.wait()
            k = n % 2
            value = dot_tn(r.a_buf[k].reshape(4 * SEQ, D), r.b_buf[k].reshape(4 * SEQ, D))
            r.prod[...] = value.reshape(16, 48, D)
            (c_split if item[0] == BLOCK else d_split)(item[1])
        for fn, args in plan.get(n, ()):
            fn(*args)
    small_out()


def run_weights(operands):
    any_space, vmem = pl.BlockSpec(memory_space=pl.ANY), pl.BlockSpec(memory_space=pltpu.VMEM)
    shapes = [(48, 3 * D), (48, D), (48, FF), (192, D), (1, 48), (1, 48), (1, 192), (1, 48), (1, 48), (1, 48)]
    outs = pl.pallas_call(
        weights_kernel, out_shape=[jax.ShapeDtypeStruct(s, F32) for s in shapes],
        in_specs=[any_space] * 8 + [vmem] * 2, out_specs=[vmem] * len(shapes),
        scratch_shapes=[pltpu.VMEM(*v) for v in W_SCRATCH.values()] + [pltpu.SemaphoreType.DMA(v) for v in W_SEMS.values()],
        name="weights",
        compiler_params=pltpu.CompilerParams(collective_id=2, has_side_effects=True, vmem_limit_bytes=62 * 2**20),
    )(*operands)
    return types.SimpleNamespace(**dict(zip(W_OUT, outs)))


def weight_product(left, right):
    rows = left.shape[0] * left.shape[1]
    return lax.dot_general(
        left.reshape(rows, -1), right.reshape(rows, -1), (((0,), (0,)), ((), ())), preferred_element_type=F32
    )


def hand_over(*results):
    count = len(results)

    def kernel(*refs):
        held, sem = refs[2 * count:3 * count], refs[3 * count]
        into = [pltpu.make_async_copy(refs[n], held[n], sem.at[0, n]) for n in range(count)]
        out = [pltpu.make_async_copy(held[n], refs[count + n], sem.at[1, n]) for n in range(count)]
        for c in into:
            c.start()
        for a, b in zip(into, out):
            a.wait()
            b.start()
        for c in out:
            c.wait()

    return tuple(pl.pallas_call(
        kernel, out_shape=[jax.ShapeDtypeStruct(v.shape, v.dtype) for v in results], in_specs=[pl.BlockSpec(memory_space=pl.ANY)] * count,
        out_specs=[pl.BlockSpec(memory_space=pl.ANY)] * count,
        scratch_shapes=[pltpu.VMEM(v.shape, v.dtype) for v in results] + [pltpu.SemaphoreType.DMA((2, count))], name="hand_over",
        compiler_params=pltpu.CompilerParams(vmem_limit_bytes=63 * 2**20),
    )(*results))


def body(
    sizes, tokens, cotangent, segment_ids, feature_ids, w_qkv, w_out, gain_attn, shift_attn, w_up, bias_up, w_down, bias_down, gain_ffn, shift_ffn
):
    micro = segment_ids.shape[0]
    weights = (w_qkv[0], w_out[0], gain_attn, shift_attn, w_up[0], bias_up, w_down[0], bias_down, gain_ffn, shift_ffn)
    (h, din, sm, sbu), o = run_pipeline(tokens, cotangent, segment_ids, feature_ids, weights, micro)
    h, din = h.reshape(1, micro * SEQ, D), din.reshape(1, micro * SEQ, D)
    if sizes == (2, 16) and micro == 4:
        g = run_weights((o.x_all, o.dq, o.ctx, o.out_in, o.nl, o.up_in, o.act, o.down_in, sm, sbu))
        return hand_over(
            h, din, g.g_qkv[None], g.g_out[None], g.g_ga, g.g_sa, g.g_up[None], g.g_bu, g.g_down[None], g.g_bd, g.g_gf, g.g_sf,
        )
    sm = jnp.sum(sm, axis=1)
    sbu = jnp.sum(sbu, axis=0)
    scatter = lambda v: lax.psum_scatter(v, "dp", scatter_dimension=0, tiled=True)[None]
    g_qkv, g_out = scatter(weight_product(o.x_all, o.dq)), scatter(weight_product(o.ctx, o.out_in))
    g_up, g_down = scatter(weight_product(o.nl, o.up_in)), scatter(weight_product(o.act, o.down_in))
    return (h, din, g_qkv, g_out, scatter(sm[0]), scatter(sm[1]), g_up, scatter(sbu), g_down, scatter(sm[2]), scatter(sm[3]), scatter(sm[4]))


def solution(mesh):
    rows, mat, vec = PartitionSpec("dp", None), PartitionSpec("section", None, None), PartitionSpec("section", None)
    in_specs = (rows,) * 4 + (mat, mat, vec, vec, mat, vec, mat, vec, vec, vec)
    big, small = PartitionSpec("section", "dp", None), PartitionSpec("section", "dp")
    out_specs = (big, big, big, big, small, small, big, small, big, small, small, small)
    return jax.shard_map(
        functools.partial(body, (mesh.shape["section"], mesh.shape["dp"])), mesh=mesh, in_specs=in_specs, out_specs=out_specs, check_vma=False
    )
```

```python
import functools
import types

import jax
import jax.numpy as jnp
from jax import lax
from jax.experimental import pallas as pl
from jax.experimental.pallas import tpu as pltpu
from jax.sharding import PartitionSpec

BF, F32 = jnp.bfloat16, jnp.float32
SEQ, D, FF, HEAD = 512, 768, 3072, 64
QB, NQ, KW = 128, 4, 384
QUADS, QW = 3, 256
FC, RB = 512, 256
EPS = 1e-5
C0, C1 = 0.7978845608028654, 0.044715
MESH = pl.DeviceIdType.MESH


def dot(a, b):
    return lax.dot_general(a, b, (((1,), (0,)), ((), ())), preferred_element_type=F32)


def dot_nt(a, b):
    return lax.dot_general(a, b, (((1,), (1,)), ((), ())), preferred_element_type=F32)


def dot_tn(a, b):
    return lax.dot_general(a, b, (((0,), (0,)), ((), ())), preferred_element_type=F32)


def keys_of(block, reach):
    return max(0, block * QB - reach), min(SEQ, (block + 1) * QB + reach)


REACH = (16, 128)


def row_blocks(size=RB):
    return [slice(n * size, (n + 1) * size) for n in range(SEQ // size)]


def norm_rows(v):
    c = v - jnp.mean(v, axis=-1, keepdims=True)
    r = lax.rsqrt(jnp.mean(c * c, axis=-1, keepdims=True) + EPS)
    return c * r, r


def norm_back(e, n, r):
    return r * (e - jnp.mean(e, axis=-1, keepdims=True) - n * jnp.mean(e * n, axis=-1, keepdims=True))


def column_sums(v):
    return jnp.sum(v.reshape(v.shape[0] // 8, 8, v.shape[1]), axis=0)


def make_bias(seg, feat, bias, reach, use_feat):
    row = (seg * 128 + feat * use_feat).astype(F32)
    col = jnp.transpose(jnp.broadcast_to(row, (QB, SEQ)))
    for qb in range(NQ):
        lo, hi = keys_of(qb, reach)
        same = col[lo:hi, :] == row[:, qb * QB:(qb + 1) * QB]
        bias[qb, 0:hi - lo, :] = jnp.where(same, 0.0, -1e30).astype(F32)


def head_lanes():
    lane = lax.broadcasted_iota(jnp.int32, (1, QW), 1)
    return [jnp.where((lane >= HEAD * i) & (lane < HEAD * (i + 1)), 1.0, 0.0).astype(BF) for i in range(4)]


def by_head(v, masks):
    return jnp.concatenate([v * m for m in masks], axis=0)


def f_qkv(x, w_qkv, qkv):
    qkv[:, 0:D] = (dot(x[...], w_qkv[:, 0:D]) * 0.125).astype(BF)
    for j in range(1, 3):
        qkv[:, j * D:(j + 1) * D] = dot(x[...], w_qkv[:, j * D:(j + 1) * D]).astype(BF)


def f_attention(qkv, bias, probs, ctx, inv, reach):
    first = lax.broadcasted_iota(jnp.int32, (QB, 128), 1) < HEAD
    masks = head_lanes()
    ones = jnp.ones((KW, 128), BF)

    def quad(p, carry):
        base = pl.multiple_of(p * QW, QW)
        scores = {}

        def begin(qb):
            lo, hi = keys_of(qb, reach)
            q = qkv[qb * QB:(qb + 1) * QB, pl.ds(base, QW)]
            k = qkv[lo:hi, pl.ds(pl.multiple_of(D + base, QW), QW)]
            scores[qb] = dot_nt(k, by_head(q, masks))

        def finish(qb):
            lo, hi = keys_of(qb, reach)
            kw, qs = hi - lo, slice(qb * QB, (qb + 1) * QB)
            v = qkv[lo:hi, pl.ds(pl.multiple_of(2 * D + base, QW), QW)]
            all_four, b, e = scores.pop(qb), bias[qb, 0:kw, :], []
            for hd in range(4):
                s = all_four[:, hd * QB:(hd + 1) * QB] + b
                e.append(jnp.exp((s - jnp.max(s, axis=0, keepdims=True)).astype(BF)))
                probs[p, qb, 0:kw, hd * QB:(hd + 1) * QB] = e[hd]
            for n in range(2):
                right = jnp.concatenate([v[:, n * 128:(n + 1) * 128], ones[:kw]], axis=1)
                o = dot_tn(jnp.concatenate(e[2 * n:2 * n + 2], axis=1), right)
                value = jnp.where(first, o[:QB, :128], o[QB:, :128])
                recip = 1.0 / jnp.where(first, o[:QB, 128:], o[QB:, 128:])
                inv[qs, pl.ds(base + n * 128, 128)] = recip
                ctx[qs, pl.ds(base + n * 128, 128)] = (value * recip).astype(BF)

        begin(0)
        begin(1)
        for qb in range(NQ):
            if qb + 2 < NQ:
                begin(qb + 2)
            finish(qb)
        return carry

    lax.fori_loop(0, QUADS, quad, 0)


def f_mid(x, ctx, w_out, gain, shift, n1, nl, r1, nf):
    for rs in row_blocks():
        n, r = norm_rows(x[rs, :].astype(F32) + dot(ctx[rs, :], w_out[...]))
        out = n * gain[...] + shift[...]
        n1[rs, :] = n.astype(BF)
        r1[rs, :] = jnp.broadcast_to(r, (RB, 128))
        nl[rs, :] = out.astype(BF)
        nf[rs, :] = out


def gelu_both(p):
    p2 = p * p
    t = jnp.tanh(p * (C0 + (C0 * C1) * p2))
    h = 0.5 + 0.5 * t
    return p * h, h + (p * (C0 + (3 * C0 * C1) * p2)) * (0.5 - 0.5 * (t * t))


def f_ffn(nl, nf, w_up, b_up, w_down, b_down, gain, shift, dg, act, n2, r2, h):
    for c in range(FF // FC):
        cs = slice(c * FC, (c + 1) * FC)
        a, d = gelu_both(dot(nl[...], w_up[:, cs]) + b_up[:, cs])
        act[:, cs] = a.astype(BF)
        dg[:, cs] = d.astype(BF)
    for rs in row_blocks():
        n, r = norm_rows(nf[rs, :] + dot(act[rs, :], w_down[...]) + b_down[...])
        n2[rs, :] = n.astype(BF)
        r2[rs, :] = jnp.broadcast_to(r, (RB, 128))
        h[rs, :] = (n * gain[...] + shift[...]).astype(BF)


def b_ffn(g, n2, r2, gain_ffn, w_down, dg, w_up, n1, r1, gain_attn, down_in, up_in, d_ffn, d_attn, out_in, sm, sbu):
    for rs in row_blocks():
        grad, n, r = g[rs, :].astype(F32), n2[rs, :].astype(F32), r2[rs, 0:1]
        d = norm_back(grad * gain_ffn[...], n, r)
        low = d.astype(BF)
        down_in[rs, :] = low
        d_ffn[rs, :] = d
        sm[3] += column_sums(grad * n)
        sm[4] += column_sums(grad)
        sm[2] += column_sums(low.astype(F32))
    for c in range(FF // FC):
        cs = slice(c * FC, (c + 1) * FC)
        u = (dot_nt(down_in[...], w_down[cs, :]) * dg[:, cs].astype(F32)).astype(BF)
        up_in[:, cs] = u
        sbu[:, cs] += column_sums(u.astype(F32))
    for rs in row_blocks():
        grad = d_ffn[rs, :] + dot_nt(up_in[rs, :], w_up[...])
        n, r = n1[rs, :].astype(F32), r1[rs, 0:1]
        d = norm_back(grad * gain_attn[...], n, r)
        d_attn[rs, :] = d
        out_in[rs, :] = d.astype(BF)
        sm[0] += column_sums(grad * n)
        sm[1] += column_sums(grad)


def b_attention(qkv, probs, ctx, d_ctx, d_qkv, reach):
    first = lax.broadcasted_iota(jnp.int32, (QB, 128), 1) < HEAD
    masks = head_lanes()
    pick = jnp.where(lax.broadcasted_iota(jnp.int32, (8, QW), 1) // HEAD == lax.broadcasted_iota(jnp.int32, (8, QW), 0), 1.0, 0.0).astype(BF)
    edges = sorted({e for qb in range(NQ) for e in keys_of(qb, reach)})

    def quad(p, carry):
        base = pl.multiple_of(p * QW, QW)
        kb, vb = pl.multiple_of(D + base, QW), pl.multiple_of(2 * D + base, QW)
        both = (d_ctx[:, pl.ds(base, QW)].astype(F32) * ctx[:, pl.ds(base, QW)].astype(F32)).astype(BF)
        delta = dot_nt(pick, both)
        d_prob, d_k, d_v = {}, {}, {}

        def begin(qb):
            lo, hi = keys_of(qb, reach)
            do = d_ctx[qb * QB:(qb + 1) * QB, pl.ds(base, QW)]
            d_prob[qb] = dot_nt(qkv[lo:hi, pl.ds(vb, QW)], by_head(do, masks))

        def finish(qb):
            lo, hi = keys_of(qb, reach)
            kw, qs = hi - lo, slice(qb * QB, (qb + 1) * QB)
            all_four, e, ds = d_prob.pop(qb), probs[p, qb, 0:kw, :], []
            for hd in range(4):
                hs = slice(hd * QB, (hd + 1) * QB)
                ds.append((e[:, hs].astype(F32) * (all_four[:, hs] - delta[hd:hd + 1, qs])).astype(BF))
            ds = jnp.concatenate(ds, axis=1)
            d_v[qb] = dot(e, by_head(d_ctx[qs, pl.ds(base, QW)], masks))
            d_k[qb] = dot(ds, by_head(qkv[qs, pl.ds(base, QW)], masks))
            k = qkv[lo:hi, pl.ds(kb, QW)]
            for n in range(2):
                o = dot_tn(ds[:, n * 2 * QB:(n + 1) * 2 * QB], k[:, n * 128:(n + 1) * 128])
                d_qkv[qs, pl.ds(base + n * 128, 128)] = (jnp.where(first, o[:QB], o[QB:]) * 0.125).astype(BF)

        def flush(done):
            low = keys_of(done, reach)[0]
            high = keys_of(done + 1, reach)[0] if done + 1 < NQ else SEQ
            for a, b in zip(edges, edges[1:]):
                if low <= a and b <= high:
                    for parts, col in ((d_k, kb), (d_v, vb)):
                        pieces = [parts[n][a - keys_of(n, reach)[0]:b - keys_of(n, reach)[0]] for n in parts if keys_of(n, reach)[0] <= a and b <= keys_of(n, reach)[1]]
                        d_qkv[a:b, pl.ds(col, QW)] = functools.reduce(lambda v, w: v + w, pieces).astype(BF)

        begin(0)
        begin(1)
        for qb in range(NQ):
            if qb + 2 < NQ:
                begin(qb + 2)
            finish(qb)
            flush(qb)
        return carry

    lax.fori_loop(0, QUADS, quad, 0)


def b_input(d_qkv, w_qkv, d_attn, d_in):
    for rs in row_blocks():
        d_in[rs, :] = (d_attn[rs, :] + dot_nt(d_qkv[rs, :], w_qkv[...])).astype(BF)


def arrays(**named):
    return named


SAVED = arrays(
    qkv=((SEQ, 3 * D), BF), probs=((QUADS, NQ, KW, 4 * QB), BF), ctx=((SEQ, D), BF), inv=((SEQ, D), F32), n1=((SEQ, D), BF), r1=((SEQ, 128), F32),
    nl=((SEQ, D), BF), dg=((SEQ, FF), BF), act=((SEQ, FF), BF), n2=((SEQ, D), BF), r2=((SEQ, 128), F32),
)
ROWS = arrays(down_in=((SEQ, D), BF), up_in=((SEQ, FF), BF), out_in=((SEQ, D), BF), dq=((SEQ, 3 * D), BF))
EARLY_BOTH, EARLY_ONE = tuple(arrays(ctx=0, nl=0)), tuple(arrays(qkv=0, probs=0, inv=0, n1=0, r1=0))
LATE_ONE = tuple(arrays(dg=0, n2=0, r2=0))
RELOADED = tuple(k for k in SAVED if k not in tuple(arrays(nl=0, act=0)))
WEIGHTS = arrays(wqkv=((D, 3 * D), BF), wout=((D, D), BF), wup=((D, FF), BF), wdown=((FF, D), BF))
INPUTS = arrays(tokens=0, cot=0, seg=0, feat=0, ga=0, sa=0, bu=0, bd=0, gf=0, sf=0)
SCRATCH = arrays(
    io=((8, SEQ, D), BF), nf=((SEQ, D), F32), datt=((SEQ, D), F32), dctx=((SEQ, D), BF), ho=((SEQ, D), BF), din=((SEQ, D), BF),
    bias=((4, NQ, KW, QB), F32), **WEIGHTS, **SAVED, **ROWS,
)
SEMS = arrays(s_w=(4,), s_own=(2,), s_f=(len(SAVED),), s_l=(len(SAVED),), s_b=(len(ROWS),), s_x=(1,), s_ho=(1,), s_din=(1,), s_sh=(1,), s_sd=(1,), s_r=(4,))


def pipeline_kernel(micro, *refs):
    n_in, n_w, n_out = len(INPUTS), len(WEIGHTS), 5 + len(SAVED) + len(ROWS)
    r = types.SimpleNamespace(**dict(zip(INPUTS, refs)))
    w_hbm = dict(zip(WEIGHTS, refs[n_in:]))
    h_all, din_all, sm, sbu, x_all = refs[n_in + n_w:][:5]
    kept = dict(zip((*SAVED, *ROWS), refs[n_in + n_w + 5:]))
    scratch = dict(zip((*SCRATCH, *SEMS), refs[n_in + n_w + n_out:]))
    s = types.SimpleNamespace(**scratch)
    sec, dp = lax.axis_index("section"), lax.axis_index("dp")
    core = lax.rem(dp, 2)
    first_sec = sec == 0
    second_sec = jnp.logical_not(first_sec)
    partner = (1 - sec, dp)
    barrier = pltpu.get_barrier_semaphore()
    pl.semaphore_signal(barrier, inc=1, device_id=partner, device_id_type=MESH)

    def own_copy(src, part):
        rows = (pl.ds(0, 1), pl.ds(1, micro - 1))[part]
        return pltpu.make_async_copy(src.at[rows], s.io.at[rows], s.s_own.at[part])

    w_copies = [pltpu.make_async_copy(w_hbm[k], scratch[k], s.s_w.at[n]) for n, k in enumerate(WEIGHTS)]

    @pl.when(first_sec)
    def _():
        own_copy(r.tokens, 0).start()

    @pl.when(second_sec)
    def _():
        own_copy(r.cot, 0).start()

    for c in w_copies:
        c.start()

    @pl.when(first_sec)
    def _():
        own_copy(r.tokens, 1).start()

    @pl.when(second_sec)
    def _():
        own_copy(r.cot, 1).start()

    sm[...] = jnp.zeros_like(sm)
    sbu[...] = jnp.zeros_like(sbu)

    def bias_of(mb, reach):
        make_bias(r.seg[pl.ds(mb, 1), :], r.feat[pl.ds(mb, 1), :], s.bias.at[mb], reach, 1 if reach == REACH[0] else 0)

    @pl.when(first_sec)
    def _():
        bias_of(0, REACH[0])

    @pl.when(second_sec)
    def _():
        lax.fori_loop(0, micro, lambda mb, c: (bias_of(mb, REACH[1]), c)[1], 0)

    own_copy(r.tokens, 0).wait()
    w_copies[0].wait()
    pl.semaphore_wait(barrier, 1)

    order = tuple(SAVED)

    def save(k, mb):
        return pltpu.make_async_copy(scratch[k], kept[k].at[mb], s.s_f.at[order.index(k)])

    def load(k, mb):
        return pltpu.make_async_copy(kept[k].at[mb], scratch[k], s.s_l.at[order.index(k)])

    def save_rows(k, mb):
        return pltpu.make_async_copy(scratch[k], kept[k].at[mb], s.s_b.at[tuple(ROWS).index(k)])

    def save_x(mb):
        return pltpu.make_async_copy(s.io.at[mb + micro * sec], x_all.at[mb], s.s_x.at[0])

    def save_act(mb):
        return save(order[8], mb)

    def save_h(mb):
        return pltpu.make_async_copy(s.ho, h_all.at[mb], s.s_ho.at[0])

    def save_din(mb):
        return pltpu.make_async_copy(s.din, din_all.at[mb], s.s_din.at[0])

    def send(src, mb, sem):
        return pltpu.make_async_remote_copy(
            src_ref=src, dst_ref=s.io.at[micro + mb], send_sem=sem.at[0], recv_sem=s.s_r.at[mb], device_id=partner, device_id_type=MESH
        )

    def send_h(mb):
        return send(s.ho, mb, s.s_sh)

    def send_din(mb):
        return send(s.din, mb, s.s_sd)

    def step(t, carry):
        is_f = jnp.where(first_sec, t < micro, lax.rem(t, 2) == 0)
        mb = jnp.where(first_sec, lax.rem(t, micro), lax.div(t, 2))
        after_f = jnp.where(first_sec, (t >= 1) & (t <= micro), lax.rem(t, 2) == 1)
        prev = jnp.where(first_sec, lax.rem(t + micro - 1, micro), lax.div(t, 2))
        late_send = first_sec & (core == 1)

        def wait_late():
            save_act(prev).wait()
            save_h(prev).wait()

            @pl.when(first_sec)
            def _():
                for k in LATE_ONE:
                    save(k, prev).wait()
                send_h(prev).wait_send()

        @pl.when(t == 1)
        def _():
            own_copy(r.tokens, 1).wait()

        @pl.when(after_f)
        def _():
            for k in EARLY_BOTH:
                save(k, prev).wait()
            save_x(prev).wait()

            @pl.when(first_sec)
            def _():
                for k in EARLY_ONE:
                    save(k, prev).wait()

        @pl.when(is_f)
        def _():
            @pl.when(second_sec)
            def _():
                send_h(mb).wait_recv()

            save_x(mb).start()
            x = s.io.at[mb + micro * sec]
            f_qkv(x, s.wqkv, s.qkv)

            @pl.when(first_sec)
            def _():
                save(order[0], mb).start()
                f_attention(s.qkv, s.bias.at[mb], s.probs, s.ctx, s.inv, REACH[0])
                for k in EARLY_ONE[1:3]:
                    save(k, mb).start()

            @pl.when(second_sec)
            def _():
                f_attention(s.qkv, s.bias.at[mb], s.probs, s.ctx, s.inv, REACH[1])

            save(EARLY_BOTH[0], mb).start()

            @pl.when(t == 0)
            def _():
                for c in w_copies[1:]:
                    c.wait()

            f_mid(x, s.ctx, s.wout, r.ga, r.sa, s.n1, s.nl, s.r1, s.nf)
            save(EARLY_BOTH[1], mb).start()

            @pl.when(late_send & (t == 1))
            def _():
                send_h(0).start()

            @pl.when(first_sec)
            def _():
                for k in EARLY_ONE[3:]:
                    save(k, mb).start()

            @pl.when(after_f)
            def _():
                wait_late()

            f_ffn(s.nl, s.nf, s.wup, r.bu, s.wdown, r.bd, r.gf, r.sf, s.dg, s.act, s.n2, s.r2, s.ho)

            @pl.when(first_sec & jnp.logical_not(late_send & (t == 0)))
            def _():
                send_h(mb).start()

            save_act(mb).start()
            save_h(mb).start()

            @pl.when(first_sec)
            def _():
                for k in LATE_ONE:
                    save(k, mb).start()

                @pl.when(t < micro - 1)
                def _():
                    bias_of(mb + 1, REACH[0])

        @pl.when(jnp.logical_not(is_f))
        def _():
            @pl.when(first_sec)
            def _():
                @pl.when(after_f)
                def _():
                    wait_late()
                    for k in RELOADED:
                        load(k, mb).start()

                for k in RELOADED:
                    load(k, mb).wait()
                send_din(mb).wait_recv()

            not_first_b = jnp.where(first_sec, t > micro, t > 1)
            before = mb - 1

            @pl.when(not_first_b)
            def _():
                for k in ROWS:
                    save_rows(k, before).wait()
                save_din(before).wait()

                @pl.when(second_sec)
                def _():
                    send_din(before).wait_send()

            g = s.io.at[mb + micro * (1 - sec)]
            b_ffn(g, s.n2, s.r2, r.gf, s.wdown, s.dg, s.wup, s.n1, s.r1, r.ga, s.down_in, s.up_in, s.nf, s.datt, s.out_in, sm, sbu)
            for k in tuple(ROWS)[:3]:
                save_rows(k, mb).start()

            @pl.when(second_sec)
            def _():
                wait_late()

            s.dctx[...] = (dot_nt(s.out_in[...], s.wout[...]) * s.inv[...]).astype(BF)

            @pl.when(first_sec)
            def _():
                b_attention(s.qkv, s.probs, s.ctx, s.dctx, s.dq, REACH[0])

            @pl.when(second_sec)
            def _():
                b_attention(s.qkv, s.probs, s.ctx, s.dctx, s.dq, REACH[1])

            save_rows(tuple(ROWS)[3], mb).start()
            b_input(s.dq, s.wqkv, s.datt, s.din)

            @pl.when(second_sec)
            def _():
                send_din(mb).start()

            save_din(mb).start()

            @pl.when(first_sec & (mb < micro - 1))
            def _():
                for k in RELOADED:
                    load(k, mb + 1).start()

        return carry

    lax.fori_loop(0, 2 * micro, step, 0)
    last = micro - 1
    for k in ROWS:
        save_rows(k, last).wait()
    save_din(last).wait()

    @pl.when(second_sec)
    def _():
        send_din(last).wait_send()


def run_pipeline(tokens, cot, seg, feat, weights, micro):
    w_qkv, w_out, gain_attn, shift_attn, w_up, bias_up, w_down, bias_down, gain_ffn, shift_ffn = weights
    any_space, vmem = pl.BlockSpec(memory_space=pl.ANY), pl.BlockSpec(memory_space=pltpu.VMEM)
    operands = (
        tokens.reshape(micro, SEQ, D), cot.reshape(micro, SEQ, D), seg, feat,
        gain_attn, shift_attn, bias_up, bias_down, gain_ffn, shift_ffn, w_qkv, w_out, w_up, w_down,
    )
    in_specs = [any_space] * 2 + [vmem] * 8 + [any_space] * 4
    out_shape = [
        jax.ShapeDtypeStruct((micro, SEQ, D), BF), jax.ShapeDtypeStruct((micro, SEQ, D), BF),
        jax.ShapeDtypeStruct((5, 8, D), F32), jax.ShapeDtypeStruct((8, FF), F32), jax.ShapeDtypeStruct((micro, SEQ, D), BF),
    ] + [jax.ShapeDtypeStruct((micro,) + shape, dtype) for shape, dtype in (*SAVED.values(), *ROWS.values())]
    out_specs = [any_space] * 2 + [vmem] * 2 + [any_space] * (len(out_shape) - 4)
    scratch = [pltpu.VMEM(*v) for v in SCRATCH.values()] + [pltpu.SemaphoreType.DMA(v) for v in SEMS.values()]
    outs = pl.pallas_call(
        functools.partial(pipeline_kernel, micro), out_shape=out_shape, in_specs=in_specs, out_specs=out_specs, scratch_shapes=scratch,
        name="pipeline",
        compiler_params=pltpu.CompilerParams(collective_id=1, has_side_effects=True, vmem_limit_bytes=63 * 2**20),
    )(*operands)
    return outs[:4], types.SimpleNamespace(x_all=outs[4], **dict(zip((*SAVED, *ROWS), outs[5:])))


WAITS, Z_WAITS, D_WAITS, LAST = (1, 6, 7, 8, 20), (1, 3, 6, 12, 20), (1, 4, 7, 11), 20
Z_FIRST = (0, 1)
BLOCK, ROW_SET = 0, 1
ITEMS = (
    (ROW_SET, 1), (BLOCK, 1), (BLOCK, 2), (BLOCK, 4), (BLOCK, 0), (ROW_SET, 3), (ROW_SET, 0), (ROW_SET, 2), (BLOCK, 5), (BLOCK, 7), (BLOCK, 6), (BLOCK, 3),
)
W_IN = arrays(x_all=0, dq=0, ctx=0, out_in=0, nl=0, up_in=0, act=0, down_in=0, sm=0, sbu=0)
W_OUT = arrays(g_qkv=0, g_out=0, g_up=0, g_down=0, g_ga=0, g_sa=0, g_bu=0, g_bd=0, g_gf=0, g_sf=0)
NC = 8
W_SCRATCH = arrays(
    a_buf=((2, 4, SEQ, D), BF), b_buf=((2, 4, SEQ, D), BF), prod=((16, 48, D), F32),
    c_send=((NC, 4, 2, 48, D), BF), c_own=((NC, 4, 2, 48, D), BF), c_r0=((NC, 4, 2, 48, D), BF),
    c_r1=((NC, 4, 48, D), BF), c_u=((NC, 4, 48, D), BF), c_r2=((NC, 2, 4, 48, D), BF),
    d_send=((4, 2, 192, D), BF), d_own=((4, 2, 192, D), BF), d_r0=((4, 2, 192, D), BF),
    d_r1=((4, 192, D), BF), d_u=((4, 192, D), BF), d_r2=((2, 4, 192, D), BF),
    z_r2=((2, 2, 4, 2, 48, D), BF), z_v=((2, 48, D), BF), z_r4=((2, 48, D), BF),
    small=((5, 16, D), F32), small_r=((4, 16, D), F32),
)
W_SEMS = arrays(
    l_a=(2,), l_b=(2,), cs0=(NC,), cr0=(NC,), cs1=(NC,), cr1=(NC,), cs2=(NC, 2, 4), cr2=(NC, 2, 4),
    ds0=(4,), dr0=(4,), ds1=(4,), dr1=(4,), ds2=(2, 4), dr2=(2, 4), ss=(4,), sr=(4,), zs4=(2,), zr4=(2,),
)


def weights_kernel(*refs):
    r = types.SimpleNamespace(**dict(zip((*W_IN, *W_OUT, *W_SCRATCH, *W_SEMS), refs)))
    sec, dp = lax.axis_index("section"), lax.axis_index("dp")
    core, y, z = lax.rem(dp, 2), lax.rem(lax.div(dp, 2), 2), lax.div(dp, 4)
    oc, oy = 1 - core, 1 - y
    at = lambda c_, y_, z_: (sec, z_ * 4 + y_ * 2 + c_)
    to_core, to_y = at(oc, y, z), at(core, oy, z)
    to_z1, to_z2 = at(core, y, z + 1 - 2 * lax.rem(z, 2)), at(core, y, lax.rem(z + 2, 4))
    end_z, mid_z = (z == 0) | (z == 3), (z == 1) | (z == 2)
    barrier = pltpu.get_barrier_semaphore()
    for peer in (to_core, to_y, at(core, y, lax.rem(z + 1, 4)), to_z2, at(core, y, lax.rem(z + 3, 4))):
        pl.semaphore_signal(barrier, inc=1, device_id=peer, device_id_type=MESH)

    def send(src, dst, s, q, peer):
        return pltpu.make_async_remote_copy(src_ref=src, dst_ref=dst, send_sem=s, recv_sem=q, device_id=peer, device_id_type=MESH)

    def block(ref, j):
        return ref if ref.shape[2] == D else ref.at[:, :, pl.ds(j, D)]

    def operands(item):
        i = item[1]
        if item[0] == ROW_SET:
            return block(r.act, i * D), block(r.down_in, 0)
        if i < 3:
            return block(r.x_all, 0), block(r.dq, i * D)
        if i == 3:
            return block(r.ctx, 0), block(r.out_in, 0)
        return block(r.nl, 0), block(r.up_in, (i - 4) * D)

    def loads(n):
        a, b = operands(ITEMS[n])
        k = n % 2
        return pltpu.make_async_copy(a, r.a_buf.at[k], r.l_a.at[k]), pltpu.make_async_copy(b, r.b_buf.at[k], r.l_b.at[k])

    f = lambda v: v.astype(F32)
    def c0(i):
        return send(r.c_send.at[i], r.c_r0.at[i], r.cs0.at[i], r.cr0.at[i], to_core)

    def c1(i):
        return send(r.c_own.at[i, :, oy], r.c_r1.at[i], r.cs1.at[i], r.cr1.at[i], to_y)

    def c2(i, way, t):
        src, dst = (r.c_own, r.z_r2) if i in Z_FIRST else (r.c_u, r.c_r2)
        return send(src.at[i, t], dst.at[i, way, t], r.cs2.at[i, way, t], r.cr2.at[i, way, t], at(core, y, z + 1 - 2 * way))

    def z4(i):
        return send(r.z_v.at[i], r.z_r4.at[i], r.zs4.at[i], r.zr4.at[i], to_y)

    def c_target(i):
        if i < 3:
            return r.g_qkv.at[:, pl.ds(i * D, D)]
        return r.g_out if i == 3 else r.g_up.at[:, pl.ds((i - 4) * D, D)]

    def c_split(i):
        for g in range(8):
            r.c_send[i, g // 2, g % 2] = r.prod[2 * g + oc].astype(BF)
            r.c_own[i, g // 2, g % 2] = r.prod[2 * g + core].astype(BF)
        c0(i).start()

    def c_after0(i):
        c0(i).wait()
        for g in range(8):
            r.c_own[i, g // 2, g % 2] = (f(r.c_own[i, g // 2, g % 2]) + f(r.c_r0[i, g // 2, g % 2])).astype(BF)
        if i in Z_FIRST:
            c_line1(i)
        else:
            c1(i).start()

    def c_after1(i):
        c1(i).wait()
        for g in range(4):
            r.c_u[i, g] = (f(r.c_own[i, g, y]) + f(r.c_r1[i, g])).astype(BF)
        c_line1(i)

    def c_line1(i):
        @pl.when(end_z)
        def _():
            for n in range(3):
                c2(i, jnp.where(z == 0, 0, 1), jnp.where(z == 0, 3 - n, n)).start()

    def c_pass(i, way, t):
        c2(i, way, t).wait_recv()
        if i in Z_FIRST:
            r.c_own[i, t] = (f(r.c_own[i, t]) + f(r.z_r2[i, way, t])).astype(BF)
        else:
            r.c_u[i, t] = (f(r.c_u[i, t]) + f(r.c_r2[i, way, t])).astype(BF)
        c2(i, way, t).start()

    def c_line2(i):
        @pl.when(mid_z)
        def _():
            for n in range(2):
                c_pass(i, jnp.where(z == 1, 0, 1), jnp.where(z == 1, 3 - n, n))

    def c_line3(i):
        @pl.when(mid_z)
        def _():
            c_pass(i, jnp.where(z == 2, 0, 1), jnp.where(z == 2, 3, 0))

    def c_last(i):
        got = r.z_r2 if i in Z_FIRST else r.c_r2
        parts = ((oy, r.prod.at[0]), (y, c_target(i))) if i in Z_FIRST else ((None, c_target(i)),)
        for q, out in parts:
            out[...] = f(r.c_u[i, z]) if q is None else f(r.c_own[i, z, q])

        @pl.when(z > 0)
        def _():
            c2(i, 0, z).wait_recv()
            for q, out in parts:
                out[...] += f(got[i, 0, z]) if q is None else f(got[i, 0, z, q])

        @pl.when(z < 3)
        def _():
            c2(i, 1, z).wait_recv()
            for q, out in parts:
                out[...] += f(got[i, 1, z]) if q is None else f(got[i, 1, z, q])

        if i in Z_FIRST:
            r.z_v[i] = r.prod[0].astype(BF)
            z4(i).start()

        @pl.when(end_z)
        def _():
            for n in range(3):
                c2(i, jnp.where(z == 0, 0, 1), jnp.where(z == 0, 3 - n, n)).wait_send()

        @pl.when(mid_z)
        def _():
            for n in range(2):
                c2(i, jnp.where(z == 1, 0, 1), jnp.where(z == 1, 3 - n, n)).wait_send()
            c2(i, jnp.where(z == 2, 0, 1), jnp.where(z == 2, 3, 0)).wait_send()

    def z_last(i):
        z4(i).wait()
        c_target(i)[...] += f(r.z_r4[i])

    def d0(k):
        return send(r.d_send.at[k], r.d_r0.at[k], r.ds0.at[k], r.dr0.at[k], to_core)

    def d1(t):
        return send(r.d_own.at[t, oy], r.d_r1.at[t], r.ds1.at[t], r.dr1.at[t], to_y)

    def d2(way, t):
        return send(r.d_u.at[t], r.d_r2.at[way, t], r.ds2.at[way, t], r.dr2.at[way, t], at(core, y, z + 1 - 2 * way))

    def d_split(k):
        for q in range(2):
            for p in range(4):
                rows = slice(48 * p, 48 * p + 48)
                r.d_send[k, q, rows] = r.prod[(2 * q + oc) * 4 + p].astype(BF)
                r.d_own[k, q, rows] = r.prod[(2 * q + core) * 4 + p].astype(BF)
        d0(k).start()

    def d_after0(k):
        d0(k).wait()
        for q in range(2):
            r.d_own[k, q] = (f(r.d_own[k, q]) + f(r.d_r0[k, q])).astype(BF)
        d1(k).start()

    def d_after1(t):
        d1(t).wait()
        r.d_u[t] = (f(r.d_own[t, y]) + f(r.d_r1[t])).astype(BF)

        @pl.when((z == 0) & (t > 0))
        def _():
            d2(0, t).start()

        @pl.when((z == 3) & (t < 3))
        def _():
            d2(1, t).start()

    def d_pass(way, t):
        d2(way, t).wait_recv()
        r.d_u[t] = (f(r.d_u[t]) + f(r.d_r2[way, t])).astype(BF)
        d2(way, t).start()

    def d_line2(t):
        @pl.when((z == 1) & (t > 1))
        def _():
            d_pass(0, t)

        @pl.when((z == 2) & (t < 2))
        def _():
            d_pass(1, t)

    def d_line3(t):
        @pl.when((z == 2) & (t > 2))
        def _():
            d_pass(0, t)

        @pl.when((z == 1) & (t < 1))
        def _():
            d_pass(1, t)

    def d_last():
        r.g_down[...] = f(r.d_u[z])

        @pl.when(z > 0)
        def _():
            d2(0, z).wait_recv()
            r.g_down[...] += f(r.d_r2[0, z])

        @pl.when(z < 3)
        def _():
            d2(1, z).wait_recv()
            r.g_down[...] += f(r.d_r2[1, z])

        for t in range(4):
            @pl.when(z < t)
            def _():
                d2(0, t).wait_send()

            @pl.when(z > t)
            def _():
                d2(1, t).wait_send()

    peers = (to_core, to_y, to_z1, to_z2)

    def small_send(k):
        return send(r.small.at[k], r.small_r.at[k], r.ss.at[k], r.sr.at[k], peers[k])

    def small_step(k):
        small_send(k).wait()
        r.small[k + 1] = r.small[k] + r.small_r[k]
        if k < 3:
            small_send(k + 1).start()

    def small_out():
        total = r.small[4]
        per = D // 16
        pick = lambda n, at_: jnp.where(lax.broadcasted_iota(jnp.int32, (D, n), 0) == at_ + lax.broadcasted_iota(jnp.int32, (D, n), 1), 1.0, 0.0)
        vec = lax.dot_general(total, pick(per, dp * per), (((1,), (0,)), ((), ())), precision=lax.Precision.HIGHEST, preferred_element_type=F32)
        up = lax.dot_general(total, pick(4 * per, lax.rem(dp, 4) * (4 * per)), (((1,), (0,)), ((), ())), precision=lax.Precision.HIGHEST, preferred_element_type=F32)
        for n, out in enumerate((r.g_ga, r.g_sa, r.g_bd, r.g_gf, r.g_sf)):
            out[...] = vec[n:n + 1]
        bu = jnp.zeros((1, 4 * per), F32)
        for n in range(4):
            bu = bu + jnp.where(lax.div(dp, 4) == n, 1.0, 0.0) * up[5 + n:6 + n]
        r.g_bu[...] = bu

    plan = {}

    def later(slot, fn, *args):
        plan.setdefault(slot, []).append((fn, args))

    for n, (kind, i) in enumerate(ITEMS):
        if kind == BLOCK and i in Z_FIRST:
            stages = tuple(zip((c_after0, c_line2, c_line3, c_last, z_last), Z_WAITS))
        elif kind == BLOCK:
            stages = tuple(zip((c_after0, c_after1, c_line2, c_line3, c_last), WAITS))
        else:
            stages = tuple(zip((d_after0, d_after1, d_line2, d_line3), D_WAITS))
        for fn, wait in stages:
            later(n + wait, fn, i)
    later(max(n for n, item in enumerate(ITEMS) if item[0] == ROW_SET) + LAST, d_last)
    for k in range(4):
        later(k + 1, small_step, k)

    for c in loads(0):
        c.start()
    r.small[0] = jnp.zeros((16, D), F32)
    r.small[0, 0:5] = jnp.sum(r.sm[...], axis=1)
    for n in range(4):
        r.small[0, 5 + n:6 + n] = jnp.sum(r.sbu[:, n * D:(n + 1) * D], axis=0, keepdims=True)
    pl.semaphore_wait(barrier, 5)
    small_send(0).start()
    for n in range(max(plan) + 1):
        if n < len(ITEMS):
            item = ITEMS[n]
            if n + 1 < len(ITEMS):
                for c in loads(n + 1):
                    c.start()
            for c in loads(n):
                c.wait()
            k = n % 2
            value = dot_tn(r.a_buf[k].reshape(4 * SEQ, D), r.b_buf[k].reshape(4 * SEQ, D))
            r.prod[...] = value.reshape(16, 48, D)
            (c_split if item[0] == BLOCK else d_split)(item[1])
        for fn, args in plan.get(n, ()):
            fn(*args)
    small_out()


def run_weights(operands):
    any_space, vmem = pl.BlockSpec(memory_space=pl.ANY), pl.BlockSpec(memory_space=pltpu.VMEM)
    shapes = [(48, 3 * D), (48, D), (48, FF), (192, D), (1, 48), (1, 48), (1, 192), (1, 48), (1, 48), (1, 48)]
    outs = pl.pallas_call(
        weights_kernel, out_shape=[jax.ShapeDtypeStruct(s, F32) for s in shapes],
        in_specs=[any_space] * 8 + [vmem] * 2, out_specs=[vmem] * len(shapes),
        scratch_shapes=[pltpu.VMEM(*v) for v in W_SCRATCH.values()] + [pltpu.SemaphoreType.DMA(v) for v in W_SEMS.values()],
        name="weights",
        compiler_params=pltpu.CompilerParams(collective_id=2, has_side_effects=True, vmem_limit_bytes=62 * 2**20),
    )(*operands)
    return types.SimpleNamespace(**dict(zip(W_OUT, outs)))


def weight_product(left, right):
    rows = left.shape[0] * left.shape[1]
    return lax.dot_general(
        left.reshape(rows, -1), right.reshape(rows, -1), (((0,), (0,)), ((), ())), preferred_element_type=F32
    )


def hand_over(*results):
    count = len(results)

    def kernel(*refs):
        held, sem = refs[2 * count:3 * count], refs[3 * count]
        into = [pltpu.make_async_copy(refs[n], held[n], sem.at[0, n]) for n in range(count)]
        out = [pltpu.make_async_copy(held[n], refs[count + n], sem.at[1, n]) for n in range(count)]
        for c in into:
            c.start()
        for a, b in zip(into, out):
            a.wait()
            b.start()
        for c in out:
            c.wait()

    return tuple(pl.pallas_call(
        kernel, out_shape=[jax.ShapeDtypeStruct(v.shape, v.dtype) for v in results], in_specs=[pl.BlockSpec(memory_space=pl.ANY)] * count,
        out_specs=[pl.BlockSpec(memory_space=pl.ANY)] * count,
        scratch_shapes=[pltpu.VMEM(v.shape, v.dtype) for v in results] + [pltpu.SemaphoreType.DMA((2, count))], name="hand_over",
        compiler_params=pltpu.CompilerParams(vmem_limit_bytes=63 * 2**20),
    )(*results))


def body(
    sizes, tokens, cotangent, segment_ids, feature_ids, w_qkv, w_out, gain_attn, shift_attn, w_up, bias_up, w_down, bias_down, gain_ffn, shift_ffn
):
    micro = segment_ids.shape[0]
    weights = (w_qkv[0], w_out[0], gain_attn, shift_attn, w_up[0], bias_up, w_down[0], bias_down, gain_ffn, shift_ffn)
    (h, din, sm, sbu), o = run_pipeline(tokens, cotangent, segment_ids, feature_ids, weights, micro)
    h, din = h.reshape(1, micro * SEQ, D), din.reshape(1, micro * SEQ, D)
    if sizes == (2, 16) and micro == 4:
        g = run_weights((o.x_all, o.dq, o.ctx, o.out_in, o.nl, o.up_in, o.act, o.down_in, sm, sbu))
        return hand_over(
            h, din, g.g_qkv[None], g.g_out[None], g.g_ga, g.g_sa, g.g_up[None], g.g_bu, g.g_down[None], g.g_bd, g.g_gf, g.g_sf,
        )
    sm = jnp.sum(sm, axis=1)
    sbu = jnp.sum(sbu, axis=0)
    scatter = lambda v: lax.psum_scatter(v, "dp", scatter_dimension=0, tiled=True)[None]
    g_qkv, g_out = scatter(weight_product(o.x_all, o.dq)), scatter(weight_product(o.ctx, o.out_in))
    g_up, g_down = scatter(weight_product(o.nl, o.up_in)), scatter(weight_product(o.act, o.down_in))
    return (h, din, g_qkv, g_out, scatter(sm[0]), scatter(sm[1]), g_up, scatter(sbu), g_down, scatter(sm[2]), scatter(sm[3]), scatter(sm[4]))


def solution(mesh):
    rows, mat, vec = PartitionSpec("dp", None), PartitionSpec("section", None, None), PartitionSpec("section", None)
    in_specs = (rows,) * 4 + (mat, mat, vec, vec, mat, vec, mat, vec, vec, vec)
    big, small = PartitionSpec("section", "dp", None), PartitionSpec("section", "dp")
    out_specs = (big, big, big, big, small, small, big, small, big, small, small, small)
    return jax.shard_map(
        functools.partial(body, (mesh.shape["section"], mesh.shape["dp"])), mesh=mesh, in_specs=in_specs, out_specs=out_specs, check_vma=False
    )
```
